128 devices in a mesh: pipe: 2 (over x_hi), dp: 32 (over z, y, x_lo), tensor: 2 (over core).
Axes of the slice: x: 4 (x_hi: 2, x_lo: 2; x = x_hi * 2 + x_lo), y: 4, z: 4, core: 2. Of those that a mesh axis runs over, the one named last changes fastest.
Arguments:
- hidden_in: bfloat16 [1, 4096, 8192], P(None, 'dp', 'tensor'), may hold values from -3 to 3
- norm_gain: float32 [2, 8192], P('pipe'), may hold values from 0.1 to 1.9
- qkv_weight: bfloat16 [2, 8192, 5120], P('pipe', None, 'tensor'), may hold values from -0.0625 to 0.0625
- qkv_bias: float32 [2, 5120], P('pipe', 'tensor'), may hold values from -3 to 3
- out_weight: bfloat16 [2, 4096, 8192], P('pipe', 'tensor', 'dp'), may hold values from -0.375 to 0.375
- segment_ids: int32 [1, 4096], P(None, 'dp'), may hold values from 0 to 1, as said below
- image_start: int32 [1, 64], P(None, 'dp'), may hold values from 1 to 124, as said below
- image_height: int32 [1, 64], P(None, 'dp'), may hold values from 2 to 6
- image_width: int32 [1, 64], P(None, 'dp'), may hold values from 2 to 6
- image_count: int32 [1, 64], P(None, 'dp'), may hold values from 0 to 1
Outputs:
- phase_outputs: bfloat16 [2, 1, 4096, 8192], P('pipe', None, 'dp', 'tensor')
The draws below stay inside these ranges and needn't reach their ends.
Inputs may be any that keep to these rules, and one draw needn't show every extreme that they name: `segment_ids`: each stream's micro-batch of 128 tokens packs two sequences, ids 0 then 1, each of 40 tokens or more. `image_start`: the image's tokens, height times width of them row by row from this offset, lie inside its sequence and after the sequence's first token, also where image_count is 0.
All inputs are finite; a program needn't handle non-finite values.
Results may differ from the reference program's by a relative error of at most 0.013.
Values may be sent and summed in bfloat16 or wider, within the bound.
A program may use at most 192 MiB of HBM per device.

```python
import math
import jax
import jax.numpy as jnp
from jax import lax

D = 8192
HEADS = 32
KV = 4
HD = 128
SEQ = 128
MICRO = 1
TOKENS = 4096
QKV = 5120
QW = 4096
N_PIPE = 2
N_DP = 32
N_TENSOR = 2


def packing(key):
    subkeys = jax.random.split(key, 6)
    grid_shape = (MICRO, N_DP)
    border = jax.random.randint(subkeys[0], grid_shape, 40, SEQ - 39)
    heights = jax.random.randint(subkeys[1], grid_shape + (2,), 2, 7)
    widths = jax.random.randint(subkeys[2], grid_shape + (2,), 2, 7)
    heights = heights.at[0, 0, 0].set(6).at[0, 0, 1].set(2)
    widths = widths.at[0, 0, 0].set(6).at[0, 0, 1].set(2)
    counts = jax.random.randint(subkeys[3], grid_shape + (2,), 0, 2)
    counts = counts.at[0, 0, :].set(1)
    image_tokens = heights * widths
    first_start = jax.random.randint(subkeys[4], grid_shape, 1, border - image_tokens[..., 0] + 1)
    second_start = border + jax.random.randint(subkeys[5], grid_shape, 1, SEQ - border - image_tokens[..., 1] + 1)
    first_start = first_start.at[0, 0].set(1)
    second_start = second_start.at[0, 0].set(SEQ - 4)
    starts = jnp.stack([first_start, second_start], axis=-1)
    return (border, heights, widths, counts, starts)


def draw_segment_ids(key, part):
    border = packing(key)[0]
    counter = jnp.arange(SEQ, dtype=jnp.int32)
    segments = (counter[None, None, :] >= border[..., None]).astype(jnp.int32)
    return segments.reshape(MICRO, N_DP * SEQ)


def draw_image_start(key, part):
    return packing(key)[4].reshape(MICRO, N_DP * 2).astype(jnp.int32)


def draw_image_height(key, part):
    return packing(key)[1].reshape(MICRO, N_DP * 2).astype(jnp.int32)


def draw_image_width(key, part):
    return packing(key)[2].reshape(MICRO, N_DP * 2).astype(jnp.int32)


def draw_image_count(key, part):
    return packing(key)[3].reshape(MICRO, N_DP * 2).astype(jnp.int32)


def level_of(own_key, shape, shards, low, high):
    loudness, own = 1.0, jax.random.fold_in(own_key, 6)
    for position, parts in shards:
        draws = jnp.exp(jax.random.uniform(jax.random.fold_in(own, position), (parts,), jnp.float32, low / len(shards), high / len(shards)))
        loudness = loudness * jnp.repeat(draws, shape[position] // parts).reshape([-1 if axis == position else 1 for axis in range(len(shape))])
    return loudness


def normal_values(stream_key, extent, spread, reach, cuts=(), kind=jnp.bfloat16):
    level = level_of(stream_key, extent, cuts, -0.22, 0.18) if cuts else 1.0
    drawn = jax.random.normal(stream_key, extent, jnp.float32) * spread * level
    return jnp.minimum(jnp.maximum(drawn, -reach), reach).astype(kind)


def setup_inputs(seed: int = 0) -> dict:
    streams_of = jax.random.split(jax.random.key(seed), 11)
    hidden_in = normal_values(streams_of[0], (MICRO, TOKENS, D), 0.5, 3.0, ((1, 32), (2, 2)))
    norm_gain = jnp.clip(1.0 + 0.18 * jax.random.normal(streams_of[1], (N_PIPE, D), jnp.float32), 0.1, 1.9)
    qkv_weight = normal_values(streams_of[2], (N_PIPE, D, QKV), D ** -0.5, 0.0625, ((0, 2), (2, 2)))
    qkv_bias = normal_values(streams_of[3], (N_PIPE, QKV), 0.5, 3.0, ((0, 2), (1, 2)), jnp.float32)
    out_weight = normal_values(streams_of[4], (N_PIPE, QW, D), (QW // 16) ** -0.5, 0.375, ((0, 2), (1, 2), (2, 32)))
    segment_ids = draw_segment_ids(jax.random.fold_in(streams_of[10], 71), 0)
    image_start = draw_image_start(jax.random.fold_in(streams_of[10], 71), 0)
    image_height = draw_image_height(jax.random.fold_in(streams_of[10], 71), 0)
    image_width = draw_image_width(jax.random.fold_in(streams_of[10], 71), 0)
    image_count = draw_image_count(jax.random.fold_in(streams_of[10], 71), 0)
    return dict(hidden_in=hidden_in, norm_gain=norm_gain, qkv_weight=qkv_weight, qkv_bias=qkv_bias, out_weight=out_weight, segment_ids=segment_ids, image_start=image_start, image_height=image_height, image_width=image_width, image_count=image_count)


rope_theta = 1000000.0
epsilon = 1e-06

def rope_tables(segment, starts, heights, widths, counts):
    head_size = HD
    token_total = segment.shape[0]
    counter = jnp.arange(token_total, dtype=jnp.int32)
    slot_ids = jnp.arange(starts.shape[0], dtype=jnp.int32)
    first_index = lax.optimization_barrier(jnp.sum((segment[None, :] < slot_ids[:, None]).astype(jnp.int32), axis=1))
    member = (segment[:, None] == slot_ids[None, :]).astype(jnp.int32)

    def choose(lookup_table):
        return lax.optimization_barrier(jnp.sum(member * lookup_table[None, :], axis=1))
    begin_pos = choose(first_index)
    anchor = choose(starts)
    rows_tall = choose(heights)
    cols_broad = choose(widths)
    present = choose(counts)
    image_span = rows_tall * cols_broad * present
    offset = counter - anchor
    inside = (offset >= 0) & (offset < image_span)
    beyond = offset >= image_span
    relative = counter - begin_pos
    shifted = relative - image_span + present * jnp.maximum(rows_tall, cols_broad)
    text_pos = jnp.where(beyond, shifted, relative)
    base_pos = anchor - begin_pos
    clipped = jnp.maximum(offset, 0)
    grid_row = clipped // cols_broad
    grid_col = clipped % cols_broad
    temporal = jnp.where(inside, base_pos, text_pos).astype(jnp.float32)
    vertical = jnp.where(inside, base_pos + grid_row, text_pos).astype(jnp.float32)
    horizontal = jnp.where(inside, base_pos + grid_col, text_pos).astype(jnp.float32)
    freq_index = jnp.arange(head_size // 2, dtype=jnp.int32)
    inverse = jnp.exp(freq_index.astype(jnp.float32) * (-2.0 * math.log(rope_theta) / head_size))
    section = jnp.where(freq_index < head_size // 8, 0, jnp.where(freq_index < head_size // 8 + 3 * head_size // 16, 1, 2))
    angles = jnp.where(section[None, :] == 0, temporal[:, None] * inverse[None, :], jnp.where(section[None, :] == 1, vertical[:, None] * inverse[None, :], horizontal[:, None] * inverse[None, :]))
    doubled = jnp.concatenate([angles, angles], axis=-1)
    return (jnp.cos(doubled), jnp.sin(doubled))

def rotate(vectors, cosine, sine_table):
    half_size = vectors.shape[-1] // 2
    turned = jnp.concatenate([-vectors[..., half_size:], vectors[..., :half_size]], axis=-1)
    return vectors * cosine + turned * sine_table

def reference(hidden_in, norm_gain, qkv_weight, qkv_bias, out_weight, segment_ids, image_start, image_height, image_width, image_count):
    query_heads = HEADS // N_TENSOR
    kv_heads = KV // N_TENSOR
    group_size = query_heads // kv_heads
    query_width = query_heads * HD
    block_width = (query_heads + 2 * kv_heads) * HD
    score_scale = 1.0 / math.sqrt(HD)
    counter = jnp.arange(SEQ, dtype=jnp.int32)
    results = []
    for micro_index in range(MICRO):
        segments = segment_ids[micro_index].reshape(N_DP, SEQ)
        cosine, sine_table = jax.vmap(rope_tables)(segments, image_start[micro_index].reshape(N_DP, 2), image_height[micro_index].reshape(N_DP, 2), image_width[micro_index].reshape(N_DP, 2), image_count[micro_index].reshape(N_DP, 2))
        allowed = (counter[None, :, None] >= counter[None, None, :]) & (segments[:, :, None] == segments[:, None, :])
        residual = hidden_in[micro_index]
        layer_outputs = []
        for layer_index in range(N_PIPE):
            widened = residual.astype(jnp.float32)
            scale_row = lax.rsqrt(lax.optimization_barrier(jnp.mean(widened * widened, axis=-1, keepdims=True)) + epsilon)
            normed = (widened * scale_row * norm_gain[layer_index][None, :]).astype(jnp.bfloat16)
            projected = jnp.dot(normed, qkv_weight[layer_index], preferred_element_type=jnp.float32) + qkv_bias[layer_index][None, :]
            blocks = projected.reshape(N_DP, SEQ, N_TENSOR, block_width)
            queries = blocks[..., :query_width].reshape(N_DP, SEQ, N_TENSOR, kv_heads, group_size, HD)
            queries = rotate(queries, cosine[:, :, None, None, None, :], sine_table[:, :, None, None, None, :]).astype(jnp.bfloat16)
            key_rows = blocks[..., query_width:query_width + kv_heads * HD].reshape(N_DP, SEQ, N_TENSOR, kv_heads, HD)
            key_rows = rotate(key_rows, cosine[:, :, None, None, :], sine_table[:, :, None, None, :]).astype(jnp.bfloat16)
            values = blocks[..., query_width + kv_heads * HD:].reshape(N_DP, SEQ, N_TENSOR, kv_heads, HD).astype(jnp.bfloat16)
            scores = jnp.einsum('dstkgh,dutkh->dtkgsu', queries.astype(jnp.float32), key_rows.astype(jnp.float32), precision=lax.Precision.HIGHEST) * score_scale
            exponent = jnp.where(allowed[:, None, None, None, :, :], jnp.exp(scores), 0.0)
            weights = (exponent / lax.optimization_barrier(jnp.sum(exponent, axis=-1, keepdims=True))).astype(jnp.bfloat16)
            attended = jnp.einsum('dtkgsu,dutkh->dstkgh', weights.astype(jnp.float32), values.astype(jnp.float32), precision=lax.Precision.HIGHEST).astype(jnp.bfloat16)
            attended = attended.reshape(N_DP * SEQ, N_TENSOR * query_width)
            update = jnp.dot(attended, out_weight[layer_index], preferred_element_type=jnp.float32)
            residual = (widened + update).astype(jnp.bfloat16)
            layer_outputs.append(residual)
        results.append(jnp.stack(layer_outputs))
    return jnp.stack(results, axis=1)
```

```python
import math

import jax
import jax.numpy as jnp
from jax import lax
from jax.experimental import pallas as pl
from jax.experimental.pallas import tpu as pltpu
from jax.sharding import PartitionSpec as P

HD = 128
SEQ = 128
D = 8192
HALF = 4096
QUERY = 2048
CHUNK = 256
CHUNKS = 10
SLOTS = 8
PIECES = 4
PIECE = 512
GROUP = 8
BLOCK = 256
THETA = 1000000.0
EPSILON = 1e-06
MIB = 1 << 20
MESH = pl.DeviceIdType.MESH


def copy_to(src, dst, send, recv, device):
    return pltpu.make_async_remote_copy(
        src_ref=src,
        dst_ref=dst,
        send_sem=send,
        recv_sem=recv,
        device_id=device,
        device_id_type=MESH,
    )


def rotary_tables(seg_ref, start_ref, height_ref, width_ref, count_ref):
    row = lax.broadcasted_iota(jnp.int32, (SEQ, SEQ), 0)
    lane = lax.broadcasted_iota(jnp.int32, (SEQ, SEQ), 1)
    seg_keys = jnp.broadcast_to(seg_ref[...].astype(jnp.float32), (SEQ, SEQ))
    seg = jnp.sum(jnp.where(row == lane, seg_keys, 0.0), axis=1, keepdims=True)
    seg = jnp.broadcast_to(seg, (SEQ, SEQ))
    allowed = (row >= lane) & (seg == seg_keys)
    border = jnp.sum(jnp.where(seg_keys == 0.0, 1.0, 0.0), axis=1, keepdims=True)
    first = seg == 0.0

    def choose(ref):
        return jnp.where(
            first, ref[0, 0].astype(jnp.float32), ref[0, 1].astype(jnp.float32)
        )

    begin = jnp.where(first, 0.0, border)
    anchor = choose(start_ref)
    tall = choose(height_ref)
    broad = choose(width_ref)
    present = choose(count_ref)
    counter = row.astype(jnp.float32)
    span = tall * broad * present
    offset = counter - anchor
    inside = (offset >= 0.0) & (offset < span)
    relative = counter - begin
    shifted = relative - span + present * jnp.maximum(tall, broad)
    text = jnp.where(offset >= span, shifted, relative)
    base = anchor - begin
    clipped = jnp.maximum(offset, 0.0)
    grid_row = jnp.floor((clipped + 0.5) / broad)
    grid_col = clipped - grid_row * broad
    freq = lane % (HD // 2)
    inverse = jnp.exp(freq.astype(jnp.float32) * (-2.0 * math.log(THETA) / HD))
    moved = jnp.where(
        freq < HD // 8, 0.0, jnp.where(freq < HD // 8 + 3 * HD // 16, grid_row, grid_col)
    )
    angles = jnp.where(inside, base + moved, text) * inverse
    sine = jnp.sin(angles)
    return jnp.cos(angles), jnp.where(lane < HD // 2, -sine, sine), allowed


def kernel(
    hidden,
    gain,
    qkv,
    bias,
    out_weight,
    seg,
    start,
    height,
    width,
    count,
    out,
    wbuf,
    gathered,
    weights,
    scaled,
    squares,
    x_own,
    x_in,
    x_relay,
    total,
    part_out,
    part_in,
    sums,
    landed,
    cosine,
    sine,
    mask,
    rows,
    keys,
    values,
    w_sem,
    local_sem,
    ws,
    wr,
    a_s,
    a_r,
    x_s,
    x_r,
    p_s,
    p_r,
    c_s,
    c_r,
    r_s,
    r_r,
    f_s,
    f_r,
):
    p = lax.axis_index("pipe")
    d = lax.axis_index("dp")
    t = lax.axis_index("tensor")
    xl = d % 2
    y = (d // 2) % 4
    z = d // 8

    def at(y_, xl_):
        return (y_ % 4) * 2 + xl_

    def device(slot, pipe=p, z_=z):
        return (pipe, (z_ % 4) * 8 + slot, t)

    own = at(y, xl)
    other_core = (p, d, 1 - t)
    partner = device(at(y, 1 - xl))
    y_up, y_down = device(at(y + 1, xl)), device(at(y + 3, xl))
    z_up, z_down = device(own, z_=z + 1), device(own, z_=z + 3)
    across = device(at(y, 1 - xl), pipe=1 - p)

    def weight_copy(step):
        chunk = (step + 8) % CHUNKS
        slot = step % SLOTS
        return pltpu.make_async_copy(
            qkv.at[:, pl.ds(pl.multiple_of(chunk * CHUNK, CHUNK), CHUNK)],
            wbuf.at[slot],
            w_sem.at[slot],
        )

    for step in range(SLOTS):
        weight_copy(step).start()
    own_weights = [
        pltpu.make_async_copy(
            out_weight.at[pl.ds(k * PIECE, PIECE)], weights.at[z, k], local_sem.at[k]
        )
        for k in range(PIECES)
    ]
    for copy in own_weights:
        copy.start()

    barrier = pltpu.get_barrier_semaphore()
    pl.semaphore_signal(barrier, inc=1, device_id=other_core, device_id_type=MESH)
    for to in (z_up, z_down):
        pl.semaphore_signal(barrier, inc=1, device_id=to, device_id_type=MESH)
    for j in range(GROUP):
        slot = (own + j) % GROUP
        pl.semaphore_signal(
            barrier, inc=1, device_id=device(slot, pipe=1 - p), device_id_type=MESH
        )
        if j:
            pl.semaphore_signal(barrier, inc=1, device_id=device(slot), device_id_type=MESH)
    pl.semaphore_wait(barrier, 2 * GROUP + 2)

    def weight_up(k):
        src = out_weight.at[pl.ds(k * PIECE, PIECE)]
        return copy_to(src, weights.at[z, k], ws.at[0, k], wr.at[0, k], z_up)

    def weight_down(k):
        src = out_weight.at[pl.ds(k * PIECE, PIECE)]
        return copy_to(src, weights.at[z, k], ws.at[1, k], wr.at[1, k], z_down)

    def weight_pass_up(k):
        ref = weights.at[(z + 3) % 4, k, pl.ds(0, PIECE // 2)]
        return copy_to(ref, ref, ws.at[2, k], wr.at[2, k], z_up)

    def weight_pass_down(k):
        ref = weights.at[(z + 1) % 4, k, pl.ds(PIECE // 2, PIECE // 2)]
        return copy_to(ref, ref, ws.at[3, k], wr.at[3, k], z_down)

    for k in range(PIECES):
        weight_up(k).start()
        weight_down(k).start()

    half = SEQ // 2

    def rows_copy(k, kind):
        ref, to = {
            0: (gathered.at[k, own], partner),
            1: (gathered.at[k, own], y_up),
            2: (gathered.at[k, own], y_down),
            3: (gathered.at[k, at(y, 1 - xl)], y_up),
            4: (gathered.at[k, at(y, 1 - xl)], y_down),
            5: (gathered.at[k, at(y + 3, xl), pl.ds(0, half)], y_up),
            6: (gathered.at[k, at(y + 1, xl), pl.ds(half, half)], y_down),
            7: (gathered.at[k, at(y + 2, xl)], partner),
        }[kind]
        return copy_to(ref, ref, a_s.at[kind, k], a_r.at[kind, k], to)

    def inject(k):
        for kind in (1, 2, 0):
            rows_copy(k, kind).start()

    def pass_first(k):
        rows_copy(k, 0).wait_recv()
        rows_copy(k, 3).start()
        rows_copy(k, 4).start()
        rows_copy(k, 1).wait_recv()
        rows_copy(k, 5).start()
        rows_copy(k, 2).wait_recv()
        rows_copy(k, 6).start()

    def pass_second(k):
        rows_copy(k, 5).wait_recv()
        rows_copy(k, 6).wait_recv()
        rows_copy(k, 7).start()

    def pass_weights(k):
        weight_up(k).wait_recv()
        weight_pass_up(k).start()
        weight_down(k).wait_recv()
        weight_pass_down(k).start()

    send_hidden = copy_to(hidden, x_relay, r_s, r_r, across)
    send_x = copy_to(x_own, x_relay, r_s, r_r, across)
    pass_hidden = copy_to(x_relay, x_in, f_s, f_r, partner)
    pass_x = copy_to(x_relay, out, f_s, f_r, partner)
    load_hidden = pltpu.make_async_copy(hidden, x_own, local_sem.at[PIECES])

    @pl.when(p == 0)
    def _():
        load_hidden.start()
        send_hidden.start()

    cos, sin, allowed = rotary_tables(seg, start, height, width, count)
    cosine[...] = cos
    sine[...] = sin
    mask[...] = jnp.where(allowed, 1.0, 0.0)

    def sums_copy(slot):
        return copy_to(
            sums.at[slot], landed.at[p, own], c_s.at[slot], c_r.at[p, own], device(slot, pipe=1)
        )

    def landed_wait(layer, slot):
        pltpu.make_async_copy(
            landed.at[layer, slot], landed.at[layer, slot], c_r.at[layer, slot]
        ).wait()

    def add_update(layer, source):
        def body(slot, carry):
            for zz in range(2):
                cols = pl.ds(pl.multiple_of(zz * 2048 + slot * BLOCK, BLOCK), BLOCK)
                x_own[:, cols] = (
                    source[:, cols].astype(jnp.float32)
                    + landed[layer, slot, zz].astype(jnp.float32)
                ).astype(jnp.bfloat16)
            return carry

        lax.fori_loop(0, GROUP, body, 0)

    @pl.when(p == 0)
    def _():
        load_hidden.wait()

    @pl.when(p == 1)
    def _():
        send_hidden.wait_recv()
        pass_hidden.start()
        pass_hidden.wait_recv()
        for slot in range(GROUP):
            landed_wait(0, slot)
        add_update(0, x_in)
        send_x.start()

    def scale_body(j, square):
        cols = pl.ds(pl.multiple_of(j * 512, 512), 512)
        x = x_own[:, cols].astype(jnp.float32)
        g = gain[:, pl.ds(pl.multiple_of(t * HALF + j * 512, 512), 512)]
        scaled[t, :, cols] = (x * g).astype(jnp.bfloat16)
        x = x * x
        return square + x[:, 0:128] + x[:, 128:256] + x[:, 256:384] + x[:, 384:512]

    square = lax.fori_loop(0, HALF // 512, scale_body, jnp.zeros((SEQ, 128), jnp.float32))
    squares[t] = square
    scaled_copy = copy_to(scaled.at[t], scaled.at[t], x_s.at[0], x_r.at[0], other_core)
    squares_copy = copy_to(squares.at[t], squares.at[t], x_s.at[1], x_r.at[1], other_core)
    scaled_copy.start()
    squares_copy.start()
    squares_copy.wait_recv()
    scaled_copy.wait_recv()
    mean = jnp.sum(squares[0] + squares[1], axis=1, keepdims=True) * (1.0 / D)
    rows[...] = jnp.broadcast_to(lax.rsqrt(mean + EPSILON), (SEQ, SEQ))

    def rotated(u):
        return (u * cosine[...] + pltpu.roll(u, HD // 2, 1) * sine[...]).astype(jnp.bfloat16)

    def project(step, carry):
        slot = step % SLOTS
        chunk = (step + 8) % CHUNKS
        weight_copy(step).wait()
        u = jnp.dot(scaled[0], wbuf[slot, 0:HALF], preferred_element_type=jnp.float32)
        u += jnp.dot(scaled[1], wbuf[slot, HALF:D], preferred_element_type=jnp.float32)
        scale = rows[...]
        b = bias[:, pl.ds(pl.multiple_of(chunk * CHUNK, CHUNK), CHUNK)]
        heads = [u[:, h * HD : (h + 1) * HD] * scale + b[:, h * HD : (h + 1) * HD] for h in range(2)]

        @pl.when(step + SLOTS < CHUNKS)
        def _():
            weight_copy(step + SLOTS).start()

        @pl.when(step == 0)
        def _():
            for h in range(2):
                keys[h] = rotated(heads[h])

        @pl.when(step == 1)
        def _():
            for h in range(2):
                values[h] = heads[h].astype(jnp.bfloat16)

        @pl.when(step >= 2)
        def _():
            q_chunk = step - 2
            kv = q_chunk // 4
            for h in range(2):
                scores = lax.dot_general(
                    rotated(heads[h]),
                    keys[kv],
                    (((1,), (1,)), ((), ())),
                    preferred_element_type=jnp.float32,
                ) * (1.0 / math.sqrt(HD))
                exponent = jnp.where(mask[...] > 0.0, jnp.exp(scores), 0.0)
                weight = exponent / jnp.sum(exponent, axis=1, keepdims=True)
                attended = jnp.dot(
                    weight.astype(jnp.bfloat16), values[kv], preferred_element_type=jnp.float32
                )
                cols = pl.multiple_of((q_chunk % 2) * CHUNK + h * HD, HD)
                gathered[q_chunk // 2, own, :, pl.ds(cols, HD)] = attended.astype(jnp.bfloat16)

            @pl.when(q_chunk % 2 == 1)
            def _():
                inject(q_chunk // 2)

            @pl.when((q_chunk % 2 == 1) & (q_chunk >= 5))
            def _():
                pass_first(q_chunk // 2 - 2)

        return carry

    lax.fori_loop(0, CHUNKS, project, 0)

    def multiply(k):
        for kind in (3, 4, 7):
            rows_copy(k, kind).wait_recv()
        weight_pass_up(k).wait_recv()
        weight_pass_down(k).wait_recv()
        own_weights[k].wait()

        def body(j, carry):
            zb = (2 * (1 - t) + j // 2) % 4
            streams = pl.ds(pl.multiple_of((j % 2) * 4, 4), 4)
            part = jnp.dot(
                gathered[k, streams].reshape(4 * SEQ, PIECE),
                weights[zb, k],
                preferred_element_type=jnp.float32,
            ).reshape(4, SEQ, BLOCK)
            if k:
                part += total[zb, streams]
            if k < PIECES - 1:
                total[zb, streams] = part
            else:

                @pl.when(j < 4)
                def _():
                    part_out[j // 2, streams] = part.astype(jnp.bfloat16)

                @pl.when(j >= 4)
                def _():
                    total[zb, streams] = part

                @pl.when((j == 1) | (j == 3))
                def _():
                    part_copy(j // 2).start()

            return carry

        lax.fori_loop(0, 8, body, 0)

    def part_copy(zz):
        return copy_to(part_out.at[zz], part_in.at[zz], p_s.at[zz], p_r.at[zz], other_core)

    pass_weights(0)
    pass_weights(1)
    pass_first(2)
    pass_first(3)
    pass_weights(2)
    pass_second(0)
    pass_weights(3)
    pass_second(1)
    pass_second(2)
    multiply(0)
    pass_second(3)
    multiply(1)
    multiply(2)
    multiply(3)

    for zz in range(2):
        part_copy(zz).wait_recv()

    def finish(j, carry):
        slot = (own + 1 + j) % GROUP
        for zz in range(2):
            sums[slot, zz] = (
                total[2 * t + zz, slot] + part_in[zz, slot].astype(jnp.float32)
            ).astype(jnp.bfloat16)

        @pl.when((p == 0) | (j < GROUP - 1))
        def _():
            sums_copy(slot).start()

        return carry

    lax.fori_loop(0, GROUP, finish, 0)

    @pl.when(p == 0)
    def _():
        send_x.wait_recv()
        pass_x.start()
        for slot in range(GROUP):
            sums_copy(slot).wait_send()
        send_hidden.wait_send()
        pass_x.wait()

    @pl.when(p == 1)
    def _():
        for zz in range(2):
            landed[1, own, zz] = sums[own, zz]
        for j in range(1, GROUP):
            landed_wait(1, (own + j) % GROUP)
        send_x.wait_send()
        add_update(1, x_own)
        store = pltpu.make_async_copy(x_own, out, local_sem.at[PIECES])
        store.start()
        for j in range(1, GROUP):
            sums_copy((own + j) % GROUP).wait_send()
        pass_hidden.wait_send()
        store.wait()

    for k in range(PIECES):
        for copy in (weight_up(k), weight_down(k), weight_pass_up(k), weight_pass_down(k)):
            copy.wait_send()
        for kind in range(8):
            rows_copy(k, kind).wait_send()
    scaled_copy.wait_send()
    squares_copy.wait_send()
    for zz in range(2):
        part_copy(zz).wait_send()


def local(hidden, gain, qkv, bias, out_weight, segment, start, height, width, count):
    bf16, f32 = jnp.bfloat16, jnp.float32
    anywhere = pl.BlockSpec(memory_space=pl.ANY)
    vmem = pl.BlockSpec(memory_space=pltpu.VMEM)
    smem = pl.BlockSpec(memory_space=pltpu.SMEM)
    dma = pltpu.SemaphoreType.DMA
    result = pl.pallas_call(
        kernel,
        out_shape=jax.ShapeDtypeStruct((SEQ, HALF), bf16),
        in_specs=[anywhere, vmem, anywhere, vmem, anywhere, vmem, smem, smem, smem, smem],
        out_specs=anywhere,
        scratch_shapes=[
            pltpu.VMEM((SLOTS, D, CHUNK), bf16),
            pltpu.VMEM((PIECES, GROUP, SEQ, PIECE), bf16),
            pltpu.VMEM((4, PIECES, PIECE, BLOCK), bf16),
            pltpu.VMEM((2, SEQ, HALF), bf16),
            pltpu.VMEM((2, SEQ, 128), f32),
            pltpu.VMEM((SEQ, HALF), bf16),
            pltpu.VMEM((SEQ, HALF), bf16),
            pltpu.VMEM((SEQ, HALF), bf16),
            pltpu.VMEM((4, GROUP, SEQ, BLOCK), f32),
            pltpu.VMEM((2, GROUP, SEQ, BLOCK), bf16),
            pltpu.VMEM((2, GROUP, SEQ, BLOCK), bf16),
            pltpu.VMEM((GROUP, 2, SEQ, BLOCK), bf16),
            pltpu.VMEM((2, GROUP, 2, SEQ, BLOCK), bf16),
            pltpu.VMEM((SEQ, SEQ), f32),
            pltpu.VMEM((SEQ, SEQ), f32),
            pltpu.VMEM((SEQ, SEQ), f32),
            pltpu.VMEM((SEQ, SEQ), f32),
            pltpu.VMEM((2, SEQ, HD), bf16),
            pltpu.VMEM((2, SEQ, HD), bf16),
            dma((SLOTS,)),
            dma((PIECES + 1,)),
            dma((4, PIECES)),
            dma((4, PIECES)),
            dma((8, PIECES)),
            dma((8, PIECES)),
            dma((2,)),
            dma((2,)),
            dma((2,)),
            dma((2,)),
            dma((GROUP,)),
            dma((2, GROUP)),
            dma(()),
            dma(()),
            dma(()),
            dma(()),
        ],
        compiler_params=pltpu.CompilerParams(
            collective_id=0, has_side_effects=True, vmem_limit_bytes=61 * MIB
        ),
        name="sublayers",
    )(
        hidden[0],
        gain,
        qkv[0],
        bias,
        out_weight[0],
        segment,
        start,
        height,
        width,
        count,
    )
    return result[None, None]


def solution(mesh):
    return jax.shard_map(
        local,
        mesh=mesh,
        in_specs=(
            P(None, "dp", "tensor"),
            P("pipe", None),
            P("pipe", None, "tensor"),
            P("pipe", "tensor"),
            P("pipe", "tensor", "dp"),
            P(None, "dp"),
            P(None, "dp"),
            P(None, "dp"),
            P(None, "dp"),
            P(None, "dp"),
        ),
        out_specs=P("pipe", None, "dp", "tensor"),
        check_vma=False,
    )
```

```python
import math

import jax
import jax.numpy as jnp
from jax import lax
from jax.experimental import pallas as pl
from jax.experimental.pallas import tpu as pltpu
from jax.sharding import PartitionSpec as P

HD = 128
SEQ = 128
D = 8192
HALF = 4096
QUERY = 2048
CHUNK = 256
CHUNKS = 10
SLOTS = 8
EARLY = 4
PIECES = 4
PIECE = 512
GROUP = 8
BLOCK = 256
THETA = 1000000.0
EPSILON = 1e-06
MIB = 1 << 20
MESH = pl.DeviceIdType.MESH


def copy_to(src, dst, send, recv, device):
    return pltpu.make_async_remote_copy(
        src_ref=src,
        dst_ref=dst,
        send_sem=send,
        recv_sem=recv,
        device_id=device,
        device_id_type=MESH,
    )


def rotary_tables(seg_ref, start_ref, height_ref, width_ref, count_ref):
    row = lax.broadcasted_iota(jnp.int32, (SEQ, SEQ), 0)
    lane = lax.broadcasted_iota(jnp.int32, (SEQ, SEQ), 1)
    seg_keys = jnp.broadcast_to(seg_ref[...].astype(jnp.float32), (SEQ, SEQ))
    seg = jnp.sum(jnp.where(row == lane, seg_keys, 0.0), axis=1, keepdims=True)
    seg = jnp.broadcast_to(seg, (SEQ, SEQ))
    allowed = (row >= lane) & (seg == seg_keys)
    border = jnp.sum(jnp.where(seg_keys == 0.0, 1.0, 0.0), axis=1, keepdims=True)
    first = seg == 0.0

    def choose(ref):
        return jnp.where(
            first, ref[0, 0].astype(jnp.float32), ref[0, 1].astype(jnp.float32)
        )

    begin = jnp.where(first, 0.0, border)
    anchor = choose(start_ref)
    tall = choose(height_ref)
    broad = choose(width_ref)
    present = choose(count_ref)
    counter = row.astype(jnp.float32)
    span = tall * broad * present
    offset = counter - anchor
    inside = (offset >= 0.0) & (offset < span)
    relative = counter - begin
    shifted = relative - span + present * jnp.maximum(tall, broad)
    text = jnp.where(offset >= span, shifted, relative)
    base = anchor - begin
    clipped = jnp.maximum(offset, 0.0)
    grid_row = jnp.floor((clipped + 0.5) / broad)
    grid_col = clipped - grid_row * broad
    freq = lane % (HD // 2)
    inverse = jnp.exp(freq.astype(jnp.float32) * (-2.0 * math.log(THETA) / HD))
    moved = jnp.where(
        freq < HD // 8, 0.0, jnp.where(freq < HD // 8 + 3 * HD // 16, grid_row, grid_col)
    )
    angles = jnp.where(inside, base + moved, text) * inverse
    sine = jnp.sin(angles)
    return jnp.cos(angles), jnp.where(lane < HD // 2, -sine, sine), allowed


def kernel(
    hidden,
    gain,
    qkv,
    bias,
    out_weight,
    seg,
    start,
    height,
    width,
    count,
    out,
    wbuf,
    gathered,
    weights,
    scaled,
    squares,
    x_own,
    x_in,
    x_relay,
    total,
    part_out,
    part_in,
    sums,
    landed,
    projected,
    cosine,
    sine,
    mask,
    rows,
    keys,
    values,
    w_sem,
    local_sem,
    ws,
    wr,
    a_s,
    a_r,
    x_s,
    x_r,
    p_s,
    p_r,
    c_s,
    c_r,
    r_s,
    r_r,
    f_s,
    f_r,
):
    p = lax.axis_index("pipe")
    d = lax.axis_index("dp")
    t = lax.axis_index("tensor")
    xl = d % 2
    y = (d // 2) % 4
    z = d // 8

    def at(y_, xl_):
        return (y_ % 4) * 2 + xl_

    def device(slot, pipe=p, z_=z):
        return (pipe, (z_ % 4) * 8 + slot, t)

    own = at(y, xl)
    other_core = (p, d, 1 - t)
    partner = device(at(y, 1 - xl))
    y_up, y_down = device(at(y + 1, xl)), device(at(y + 3, xl))
    z_up, z_down = device(own, z_=z + 1), device(own, z_=z + 3)
    across = device(at(y, 1 - xl), pipe=1 - p)

    def weight_copy(step):
        chunk = (step + 8) % CHUNKS
        slot = step % SLOTS
        return pltpu.make_async_copy(
            qkv.at[:, pl.ds(pl.multiple_of(chunk * CHUNK, CHUNK), CHUNK)],
            wbuf.at[slot],
            w_sem.at[slot],
        )

    load_hidden = pltpu.make_async_copy(hidden, x_in, local_sem.at[PIECES])

    @pl.when(p == 0)
    def _():
        load_hidden.start()

    for step in range(SLOTS):
        weight_copy(step).start()
    own_weights = [
        pltpu.make_async_copy(
            out_weight.at[pl.ds(k * PIECE, PIECE)], weights.at[z, k], local_sem.at[k]
        )
        for k in range(PIECES)
    ]

    barrier = pltpu.get_barrier_semaphore()
    pl.semaphore_signal(barrier, inc=1, device_id=other_core, device_id_type=MESH)
    for to in (z_up, z_down):
        pl.semaphore_signal(barrier, inc=1, device_id=to, device_id_type=MESH)
    for j in range(GROUP):
        slot = (own + j) % GROUP
        pl.semaphore_signal(
            barrier, inc=1, device_id=device(slot, pipe=1 - p), device_id_type=MESH
        )
        if j:
            pl.semaphore_signal(barrier, inc=1, device_id=device(slot), device_id_type=MESH)

    def weight_up(k):
        src = out_weight.at[pl.ds(k * PIECE, PIECE)]
        return copy_to(src, weights.at[z, k], ws.at[0, k], wr.at[0, k], z_up)

    def weight_down(k):
        src = out_weight.at[pl.ds(k * PIECE, PIECE)]
        return copy_to(src, weights.at[z, k], ws.at[1, k], wr.at[1, k], z_down)

    def weight_pass_up(k):
        ref = weights.at[(z + 3) % 4, k, pl.ds(0, PIECE // 2)]
        return copy_to(ref, ref, ws.at[2, k], wr.at[2, k], z_up)

    def weight_pass_down(k):
        ref = weights.at[(z + 1) % 4, k, pl.ds(PIECE // 2, PIECE // 2)]
        return copy_to(ref, ref, ws.at[3, k], wr.at[3, k], z_down)

    def pass_weights(k):
        weight_up(k).wait_recv()
        weight_pass_up(k).start()
        weight_down(k).wait_recv()
        weight_pass_down(k).start()

    half = SEQ // 2

    def rows_copy(k, kind):
        ref, to = {
            0: (gathered.at[k, own], partner),
            1: (gathered.at[k, own], y_up),
            2: (gathered.at[k, own], y_down),
            3: (gathered.at[k, at(y, 1 - xl)], y_up),
            4: (gathered.at[k, at(y, 1 - xl)], y_down),
            5: (gathered.at[k, at(y + 3, xl), pl.ds(0, half)], y_up),
            6: (gathered.at[k, at(y + 1, xl), pl.ds(half, half)], y_down),
            7: (gathered.at[k, at(y + 2, xl)], partner),
        }[kind]
        return copy_to(ref, ref, a_s.at[kind, k], a_r.at[kind, k], to)

    def inject(k):
        for kind in (1, 2, 0):
            rows_copy(k, kind).start()

    def pass_first(k):
        rows_copy(k, 0).wait_recv()
        rows_copy(k, 3).start()
        rows_copy(k, 4).start()
        rows_copy(k, 1).wait_recv()
        rows_copy(k, 5).start()
        rows_copy(k, 2).wait_recv()
        rows_copy(k, 6).start()

    def pass_second(k):
        rows_copy(k, 5).wait_recv()
        rows_copy(k, 6).wait_recv()
        rows_copy(k, 7).start()

    def strip(k):
        return pl.ds(k * (SEQ // PIECES), SEQ // PIECES)

    def send_across(src, k):
        return copy_to(src.at[strip(k)], x_relay.at[strip(k)], r_s.at[k], r_r.at[k], across)

    def pass_across(dst, k):
        return copy_to(x_relay.at[strip(k)], dst.at[strip(k)], f_s.at[k], f_r.at[k], partner)

    cos, sin, allowed = rotary_tables(seg, start, height, width, count)
    cosine[...] = cos
    sine[...] = sin
    mask[...] = jnp.where(allowed, 1.0, 0.0)
    squares[t] = jnp.zeros((SEQ, 128), jnp.float32)

    def block(slot, zz):
        return pl.ds(pl.multiple_of(zz * 2048 + slot * BLOCK, BLOCK), BLOCK)

    def prepare(slot, zz, update):
        cols = block(slot, zz)
        x = x_in[:, cols]
        if update:
            x = x.astype(jnp.float32) + landed[0, slot, zz].astype(jnp.float32)
            x = x.astype(jnp.bfloat16)
        x_own[:, cols] = x
        x = x.astype(jnp.float32)
        g = gain[:, pl.ds(pl.multiple_of(t * HALF + zz * 2048 + slot * BLOCK, BLOCK), BLOCK)]
        scaled[t, :, cols] = (x * g).astype(jnp.bfloat16)
        x = x * x
        squares[t] += x[:, 0:128] + x[:, 128:256]

    def scaled_copy(slot, zz):
        ref = scaled.at[t, :, block(slot, zz)]
        return copy_to(ref, ref, x_s.at[slot, zz], x_r.at[slot, zz], other_core)

    squares_copy = copy_to(
        squares.at[t], squares.at[t], x_s.at[GROUP, 0], x_r.at[GROUP, 0], other_core
    )

    def landed_wait(layer, slot, zz):
        ref = landed.at[layer, slot, zz]
        pltpu.make_async_copy(ref, ref, c_r.at[layer, slot, zz]).wait()

    def rotated(u):
        return (u * cosine[...] + pltpu.roll(u, HD // 2, 1) * sine[...]).astype(jnp.bfloat16)

    def product(step, core):
        return jnp.dot(
            scaled[core],
            wbuf[step % SLOTS, pl.ds(pl.multiple_of(core * HALF, HALF), HALF)],
            preferred_element_type=jnp.float32,
        )

    def finished(step, u):
        cols = pl.ds(pl.multiple_of(((step + 8) % CHUNKS) * CHUNK, CHUNK), CHUNK)
        scale = rows[...]
        for h in range(2):
            lanes = slice(h * HD, (h + 1) * HD)
            projected[step, :, lanes] = u[:, lanes] * scale + bias[:, cols][:, lanes]

    def first_half(step, carry):
        weight_copy(step).wait()
        projected[step] = product(step, t)
        return carry

    def second_half(step, carry):
        finished(step, projected[step] + product(step, 1 - t))

        @pl.when(step + SLOTS < CHUNKS)
        def _():
            weight_copy(step + SLOTS).start()

        return carry

    @pl.when(p == 0)
    def _():
        load_hidden.wait()

        def body(slot, carry):
            for zz in range(2):
                prepare(slot, zz, False)
            return carry

        lax.fori_loop(0, GROUP, body, 0)
        lax.fori_loop(0, EARLY, first_half, 0)

    pl.semaphore_wait(barrier, 2 * GROUP + 2)

    @pl.when(p == 0)
    def _():
        for slot in range(GROUP):
            for zz in range(2):
                scaled_copy(slot, zz).start()
        squares_copy.start()

    for k in range(PIECES):
        weight_up(k).start()
        weight_down(k).start()
    for copy in own_weights:
        copy.start()

    @pl.when(p == 0)
    def _():
        for k in range(PIECES):
            send_across(hidden, k).start()

    @pl.when(p == 1)
    def _():
        for k in range(PIECES):
            pass_weights(k)
            send_across(hidden, k).wait_recv()
            pass_across(x_in, k).start()
        for k in range(PIECES):
            pass_across(x_in, k).wait_recv()

        def body(j, carry):
            slot = (own + j) % GROUP
            for zz in range(2):
                landed_wait(0, slot, zz)
                prepare(slot, zz, True)
                scaled_copy(slot, zz).start()
            return carry

        lax.fori_loop(0, GROUP, body, 0)
        squares_copy.start()
        for k in range(PIECES):
            send_across(x_own, k).start()

    lax.fori_loop(EARLY * (1 - p), SLOTS, first_half, 0)
    squares_copy.wait_recv()
    for slot in range(GROUP):
        for zz in range(2):
            scaled_copy(slot, zz).wait_recv()
    mean = jnp.sum(squares[0] + squares[1], axis=1, keepdims=True) * (1.0 / D)
    rows[...] = jnp.broadcast_to(lax.rsqrt(mean + EPSILON), (SEQ, SEQ))
    lax.fori_loop(0, 3, second_half, 0)
    for h in range(2):
        keys[h] = rotated(projected[0, :, h * HD : (h + 1) * HD])
        values[h] = projected[1, :, h * HD : (h + 1) * HD].astype(jnp.bfloat16)

    def attend(step):
        q_chunk = step - 2
        kv = q_chunk // 4
        for h in range(2):
            scores = lax.dot_general(
                rotated(projected[step, :, h * HD : (h + 1) * HD]),
                keys[kv],
                (((1,), (1,)), ((), ())),
                preferred_element_type=jnp.float32,
            ) * (1.0 / math.sqrt(HD))
            exponent = jnp.where(mask[...] > 0.0, jnp.exp(scores), 0.0)
            weight = exponent * (1.0 / jnp.sum(exponent, axis=1, keepdims=True))
            attended = jnp.dot(
                weight.astype(jnp.bfloat16), values[kv], preferred_element_type=jnp.float32
            )
            cols = pl.multiple_of((q_chunk % 2) * CHUNK + h * HD, HD)
            gathered[q_chunk // 2, own, :, pl.ds(cols, HD)] = attended.astype(jnp.bfloat16)

    def pass_on(q_chunk):
        @pl.when(q_chunk % 2 == 1)
        def _():
            inject(q_chunk // 2)

    def project_second(step, carry):
        attend(step - 1)
        finished(step, projected[step] + product(step, 1 - t))
        pass_on(step - 3)
        return carry

    def project_both(step, carry):
        weight_copy(step).wait()
        attend(step - 1)
        finished(step, product(step, 0) + product(step, 1))
        pass_on(step - 3)
        return carry

    lax.fori_loop(3, SLOTS, project_second, 0)
    lax.fori_loop(SLOTS, CHUNKS, project_both, 0)
    attend(CHUNKS - 1)
    inject(PIECES - 1)

    def part_copy(slot, zz):
        return copy_to(
            part_out.at[slot, zz],
            part_in.at[slot, zz],
            p_s.at[slot, zz],
            p_r.at[slot, zz],
            other_core,
        )

    def sums_copy(slot, zz):
        return copy_to(
            sums.at[slot, zz],
            landed.at[p, own, zz],
            c_s.at[slot, zz],
            c_r.at[p, own, zz],
            device(slot, pipe=1),
        )

    def nth(j):
        pair, odd = j // 2, j % 2
        along = (pair * (3 - pair)) // 2
        dy = along * (3 + 2 * odd) + 2 * (pair // 3)
        dx = (1 - along) * odd + (pair // 2) * (1 - pair // 3)
        return at(y + dy, (xl + dx) % 2)

    def unit(slot, zb):
        part = jnp.dot(gathered[0, slot], weights[zb, 0], preferred_element_type=jnp.float32)
        for k in range(1, PIECES):
            part += jnp.dot(gathered[k, slot], weights[zb, k], preferred_element_type=jnp.float32)

        @pl.when(zb // 2 == t)
        def _():
            total[slot, zb % 2] = part

        @pl.when(zb // 2 != t)
        def _():
            part_out[slot, zb % 2] = part.astype(jnp.bfloat16)
            part_copy(slot, zb % 2).start()

    def finish(slot, zb):
        zz = zb % 2

        @pl.when(zb // 2 == t)
        def _():
            part_copy(slot, zz).wait_recv()
            sums[slot, zz] = (total[slot, zz] + part_in[slot, zz].astype(jnp.float32)).astype(
                jnp.bfloat16
            )

            @pl.when((p == 0) | (slot != own))
            def _():
                sums_copy(slot, zz).start()

    def each(action, count, place):
        def body(i, carry):
            j, turn = place(i)
            action(nth(j), (z + turn) % 4)
            return carry

        lax.fori_loop(0, count, body, 0)

    def near(i):
        return i, 0

    def beside(i):
        return i // 2, 1 + 2 * (i % 2)

    def corner(i):
        return 4 + i // 3, i % 3 + (i % 3) // 2

    def facing(i):
        return 6, i + i // 2

    def far(i):
        return i, 2

    def last(i):
        return 7, i

    def pass_weights_now(k):
        @pl.when(p == 0)
        def _():
            pass_weights(k)

    pass_first(0)
    pass_weights_now(0)
    pass_first(1)
    pass_first(2)
    pass_weights_now(1)
    pass_first(3)
    for copy in own_weights:
        copy.wait()
    each(unit, 4, near)
    pass_weights_now(2)
    pass_second(0)
    each(finish, 4, near)
    pass_second(1)
    pass_weights_now(3)
    each(unit, 8, beside)
    pass_second(2)
    each(finish, 8, beside)
    pass_second(3)
    for k in range(PIECES):
        rows_copy(k, 3).wait_recv()
        rows_copy(k, 4).wait_recv()
    each(unit, 6, corner)
    each(finish, 6, corner)
    each(unit, 3, facing)
    each(finish, 3, facing)
    for k in range(PIECES):
        weight_pass_up(k).wait_recv()
        weight_pass_down(k).wait_recv()
    each(unit, 7, far)
    each(finish, 7, far)
    for k in range(PIECES):
        rows_copy(k, 7).wait_recv()
    each(unit, 4, last)
    each(finish, 4, last)

    @pl.when(p == 0)
    def _():
        for k in range(PIECES):
            send_across(x_own, k).wait_recv()
            pass_across(out, k).start()
        for slot in range(GROUP):
            for zz in range(2):
                sums_copy(slot, zz).wait_send()
        for k in range(PIECES):
            send_across(hidden, k).wait_send()
            pass_across(out, k).wait()

    @pl.when(p == 1)
    def _():
        def add(slot, zz, update):
            cols = block(slot, zz)
            out[:, cols] = (
                x_own[:, cols].astype(jnp.float32) + update.astype(jnp.float32)
            ).astype(jnp.bfloat16)

        def body(j, carry):
            slot = nth(j)
            for zz in range(2):
                landed_wait(1, slot, zz)
                add(slot, zz, landed[1, slot, zz])
            return carry

        for zz in range(2):
            add(own, zz, sums[own, zz])
        lax.fori_loop(1, GROUP, body, 0)
        for j in range(1, GROUP):
            for zz in range(2):
                sums_copy((own + j) % GROUP, zz).wait_send()
        for k in range(PIECES):
            send_across(x_own, k).wait_send()
            pass_across(x_in, k).wait_send()

    for k in range(PIECES):
        for copy in (weight_up(k), weight_down(k), weight_pass_up(k), weight_pass_down(k)):
            copy.wait_send()
        for kind in range(8):
            rows_copy(k, kind).wait_send()
    squares_copy.wait_send()
    for slot in range(GROUP):
        for zz in range(2):
            scaled_copy(slot, zz).wait_send()
            part_copy(slot, zz).wait_send()


def local(hidden, gain, qkv, bias, out_weight, segment, start, height, width, count):
    bf16, f32 = jnp.bfloat16, jnp.float32
    anywhere = pl.BlockSpec(memory_space=pl.ANY)
    vmem = pl.BlockSpec(memory_space=pltpu.VMEM)
    smem = pl.BlockSpec(memory_space=pltpu.SMEM)
    dma = pltpu.SemaphoreType.DMA
    result = pl.pallas_call(
        kernel,
        out_shape=jax.ShapeDtypeStruct((SEQ, HALF), bf16),
        in_specs=[anywhere, vmem, anywhere, vmem, anywhere, vmem, smem, smem, smem, smem],
        out_specs=vmem,
        scratch_shapes=[
            pltpu.VMEM((SLOTS, D, CHUNK), bf16),
            pltpu.VMEM((PIECES, GROUP, SEQ, PIECE), bf16),
            pltpu.VMEM((4, PIECES, PIECE, BLOCK), bf16),
            pltpu.VMEM((2, SEQ, HALF), bf16),
            pltpu.VMEM((2, SEQ, 128), f32),
            pltpu.VMEM((SEQ, HALF), bf16),
            pltpu.VMEM((SEQ, HALF), bf16),
            pltpu.VMEM((SEQ, HALF), bf16),
            pltpu.VMEM((GROUP, 2, SEQ, BLOCK), f32),
            pltpu.VMEM((GROUP, 2, SEQ, BLOCK), bf16),
            pltpu.VMEM((GROUP, 2, SEQ, BLOCK), bf16),
            pltpu.VMEM((GROUP, 2, SEQ, BLOCK), bf16),
            pltpu.VMEM((2, GROUP, 2, SEQ, BLOCK), bf16),
            pltpu.VMEM((CHUNKS, SEQ, CHUNK), f32),
            pltpu.VMEM((SEQ, SEQ), f32),
            pltpu.VMEM((SEQ, SEQ), f32),
            pltpu.VMEM((SEQ, SEQ), f32),
            pltpu.VMEM((SEQ, SEQ), f32),
            pltpu.VMEM((2, SEQ, HD), bf16),
            pltpu.VMEM((2, SEQ, HD), bf16),
            dma((SLOTS,)),
            dma((PIECES + 1,)),
            dma((4, PIECES)),
            dma((4, PIECES)),
            dma((8, PIECES)),
            dma((8, PIECES)),
            dma((GROUP + 1, 2)),
            dma((GROUP + 1, 2)),
            dma((GROUP, 2)),
            dma((GROUP, 2)),
            dma((GROUP, 2)),
            dma((2, GROUP, 2)),
            dma((PIECES,)),
            dma((PIECES,)),
            dma((PIECES,)),
            dma((PIECES,)),
        ],
        compiler_params=pltpu.CompilerParams(
            collective_id=0, has_side_effects=True, vmem_limit_bytes=61 * MIB
        ),
        name="sublayers",
    )(
        hidden[0],
        gain,
        qkv[0],
        bias,
        out_weight[0],
        segment,
        start,
        height,
        width,
        count,
    )
    return result[None, None]


def solution(mesh):
    return jax.shard_map(
        local,
        mesh=mesh,
        in_specs=(
            P(None, "dp", "tensor"),
            P("pipe", None),
            P("pipe", None, "tensor"),
            P("pipe", "tensor"),
            P("pipe", "tensor", "dp"),
            P(None, "dp"),
            P(None, "dp"),
            P(None, "dp"),
            P(None, "dp"),
            P(None, "dp"),
        ),
        out_specs=P("pipe", None, "dp", "tensor"),
        check_vma=False,
    )
```

```python
import math

import jax
import jax.numpy as jnp
from jax import lax
from jax.experimental import pallas as pl
from jax.experimental.pallas import tpu as pltpu
from jax.sharding import PartitionSpec as P

HD = 128
SEQ = 128
D = 8192
HALF = 4096
QUERY = 2048
CHUNK = 256
CHUNKS = 10
SLOTS = 8
EARLY = 4
PIECES = 4
PIECE = 512
GROUP = 8
BLOCK = 256
THETA = 1000000.0
EPSILON = 1e-06
MIB = 1 << 20
MESH = pl.DeviceIdType.MESH


def copy_to(src, dst, send, recv, device):
    return pltpu.make_async_remote_copy(
        src_ref=src,
        dst_ref=dst,
        send_sem=send,
        recv_sem=recv,
        device_id=device,
        device_id_type=MESH,
    )


def rotary_tables(seg_ref, start_ref, height_ref, width_ref, count_ref):
    row = lax.broadcasted_iota(jnp.int32, (SEQ, SEQ), 0)
    lane = lax.broadcasted_iota(jnp.int32, (SEQ, SEQ), 1)
    seg_keys = jnp.broadcast_to(seg_ref[...].astype(jnp.float32), (SEQ, SEQ))
    seg = jnp.sum(jnp.where(row == lane, seg_keys, 0.0), axis=1, keepdims=True)
    seg = jnp.broadcast_to(seg, (SEQ, SEQ))
    allowed = (row >= lane) & (seg == seg_keys)
    border = jnp.sum(jnp.where(seg_keys == 0.0, 1.0, 0.0), axis=1, keepdims=True)
    first = seg == 0.0

    def choose(ref):
        return jnp.where(
            first, ref[0, 0].astype(jnp.float32), ref[0, 1].astype(jnp.float32)
        )

    begin = jnp.where(first, 0.0, border)
    anchor = choose(start_ref)
    tall = choose(height_ref)
    broad = choose(width_ref)
    present = choose(count_ref)
    counter = row.astype(jnp.float32)
    span = tall * broad * present
    offset = counter - anchor
    inside = (offset >= 0.0) & (offset < span)
    relative = counter - begin
    shifted = relative - span + present * jnp.maximum(tall, broad)
    text = jnp.where(offset >= span, shifted, relative)
    base = anchor - begin
    clipped = jnp.maximum(offset, 0.0)
    grid_row = jnp.floor((clipped + 0.5) / broad)
    grid_col = clipped - grid_row * broad
    freq = lane % (HD // 2)
    inverse = jnp.exp(freq.astype(jnp.float32) * (-2.0 * math.log(THETA) / HD))
    moved = jnp.where(
        freq < HD // 8, 0.0, jnp.where(freq < HD // 8 + 3 * HD // 16, grid_row, grid_col)
    )
    angles = jnp.where(inside, base + moved, text) * inverse
    sine = jnp.sin(angles)
    return jnp.cos(angles), jnp.where(lane < HD // 2, -sine, sine), allowed


def kernel(
    hidden,
    gain,
    qkv,
    bias,
    out_weight,
    seg,
    start,
    height,
    width,
    count,
    out,
    wbuf,
    gathered,
    weights,
    scaled,
    squares,
    x_own,
    x_in,
    x_relay,
    total,
    part_out,
    part_in,
    sums,
    landed,
    projected,
    cosine,
    sine,
    mask,
    rows,
    keys,
    values,
    w_sem,
    local_sem,
    ws,
    wr,
    a_s,
    a_r,
    x_s,
    x_r,
    p_s,
    p_r,
    c_s,
    c_r,
    r_s,
    r_r,
    f_s,
    f_r,
):
    p = lax.axis_index("pipe")
    d = lax.axis_index("dp")
    t = lax.axis_index("tensor")
    xl = d % 2
    y = (d // 2) % 4
    z = d // 8

    def at(y_, xl_):
        return (y_ % 4) * 2 + xl_

    def device(slot, pipe=p, z_=z):
        return (pipe, (z_ % 4) * 8 + slot, t)

    own = at(y, xl)
    other_core = (p, d, 1 - t)
    partner = device(at(y, 1 - xl))
    y_up, y_down = device(at(y + 1, xl)), device(at(y + 3, xl))
    z_up, z_down = device(own, z_=z + 1), device(own, z_=z + 3)
    across = device(at(y, 1 - xl), pipe=1 - p)

    def weight_copy(step):
        chunk = (step + 8) % CHUNKS
        slot = step % SLOTS
        return pltpu.make_async_copy(
            qkv.at[:, pl.ds(pl.multiple_of(chunk * CHUNK, CHUNK), CHUNK)],
            wbuf.at[slot],
            w_sem.at[slot],
        )

    load_hidden = pltpu.make_async_copy(hidden, x_in, local_sem.at[PIECES])

    @pl.when(p == 0)
    def _():
        load_hidden.start()

    for step in range(EARLY):
        weight_copy(step).start()
    own_weights = [
        pltpu.make_async_copy(
            out_weight.at[pl.ds(k * PIECE, PIECE)], weights.at[xl, z, k], local_sem.at[k]
        )
        for k in range(PIECES)
    ]

    barrier = pltpu.get_barrier_semaphore()
    pl.semaphore_signal(barrier, inc=1, device_id=other_core, device_id_type=MESH)
    for to in (z_up, z_down):
        pl.semaphore_signal(barrier, inc=1, device_id=to, device_id_type=MESH)
    for j in range(GROUP):
        slot = (own + j) % GROUP
        pl.semaphore_signal(
            barrier, inc=1, device_id=device(slot, pipe=1 - p), device_id_type=MESH
        )
        if j:
            pl.semaphore_signal(barrier, inc=1, device_id=device(slot), device_id_type=MESH)

    def weight_up(k):
        src = out_weight.at[pl.ds(k * PIECE, PIECE)]
        return copy_to(src, weights.at[xl, z, k], ws.at[0, k], wr.at[0, k], z_up)

    def weight_down(k):
        src = out_weight.at[pl.ds(k * PIECE, PIECE)]
        return copy_to(src, weights.at[xl, z, k], ws.at[1, k], wr.at[1, k], z_down)

    def weight_pass_up(k):
        ref = weights.at[xl, (z + 3) % 4, k, pl.ds(0, PIECE // 2)]
        return copy_to(ref, ref, ws.at[2, k], wr.at[2, k], z_up)

    def weight_pass_down(k):
        ref = weights.at[xl, (z + 1) % 4, k, pl.ds(PIECE // 2, PIECE // 2)]
        return copy_to(ref, ref, ws.at[3, k], wr.at[3, k], z_down)

    def weight_over(k):
        src = out_weight.at[pl.ds(k * PIECE, PIECE)]
        return copy_to(src, weights.at[xl, z, k], ws.at[4, k], wr.at[4, k], partner)

    def weight_on(k, kind):
        ref = weights.at[1 - xl, z, k]
        return copy_to(ref, ref, ws.at[kind, k], wr.at[kind, k], z_up if kind == 5 else z_down)

    def weight_opposite(k):
        ref = weights.at[xl, (z + 2) % 4, k]
        return copy_to(ref, ref, ws.at[7, k], wr.at[7, k], partner)

    def pass_weights(k):
        weight_up(k).wait_recv()
        weight_pass_up(k).start()
        weight_down(k).wait_recv()
        weight_pass_down(k).start()

    half = SEQ // 2

    def rows_copy(k, kind):
        ref, to = {
            0: (gathered.at[k, own], partner),
            1: (gathered.at[k, own], y_up),
            2: (gathered.at[k, own], y_down),
            3: (gathered.at[k, at(y, 1 - xl)], y_up),
            4: (gathered.at[k, at(y, 1 - xl)], y_down),
            5: (gathered.at[k, at(y + 3, xl), pl.ds(0, half)], y_up),
            6: (gathered.at[k, at(y + 1, xl), pl.ds(half, half)], y_down),
            7: (gathered.at[k, at(y + 2, xl)], partner),
        }[kind]
        return copy_to(ref, ref, a_s.at[kind, k], a_r.at[kind, k], to)

    def inject(k):
        for kind in (1, 2):
            rows_copy(k, kind).start()

        @pl.when(p == 0)
        def _():
            rows_copy(k, 0).start()

    def pass_first(k):
        rows_copy(k, 0).wait_recv()
        rows_copy(k, 3).start()
        rows_copy(k, 4).start()
        pass_along(k)

    def pass_along(k):
        rows_copy(k, 1).wait_recv()
        rows_copy(k, 5).start()
        rows_copy(k, 2).wait_recv()
        rows_copy(k, 6).start()

    def pass_second(k):
        rows_copy(k, 5).wait_recv()
        rows_copy(k, 6).wait_recv()
        rows_copy(k, 7).start()

    def strip(k):
        return pl.ds(k * (SEQ // PIECES), SEQ // PIECES)

    def send_across(src, k):
        return copy_to(src.at[strip(k)], x_relay.at[strip(k)], r_s.at[k], r_r.at[k], across)

    def pass_across(dst, k):
        return copy_to(x_relay.at[strip(k)], dst.at[strip(k)], f_s.at[k], f_r.at[k], partner)

    cos, sin, allowed = rotary_tables(seg, start, height, width, count)
    cosine[...] = cos
    sine[...] = sin
    mask[...] = jnp.where(allowed, 1.0, 0.0)
    squares[t] = jnp.zeros((SEQ, 128), jnp.float32)

    def block(slot, zz):
        return pl.ds(pl.multiple_of(zz * 2048 + slot * BLOCK, BLOCK), BLOCK)

    def prepare(slot, zz, update):
        cols = block(slot, zz)
        x = x_in[:, cols]
        if update:
            x = x.astype(jnp.float32) + landed[0, slot, zz].astype(jnp.float32)
            x = x.astype(jnp.bfloat16)
        x_own[:, cols] = x
        x = x.astype(jnp.float32)
        g = gain[:, pl.ds(pl.multiple_of(t * HALF + zz * 2048 + slot * BLOCK, BLOCK), BLOCK)]
        scaled[t, :, cols] = (x * g).astype(jnp.bfloat16)
        x = x * x
        squares[t] += x[:, 0:128] + x[:, 128:256]

    def scaled_copy(slot, zz):
        ref = scaled.at[t, :, block(slot, zz)]
        return copy_to(ref, ref, x_s.at[slot, zz], x_r.at[slot, zz], other_core)

    squares_copy = copy_to(
        squares.at[t], squares.at[t], x_s.at[GROUP, 0], x_r.at[GROUP, 0], other_core
    )
    scaled_whole = copy_to(
        scaled.at[t], scaled.at[t], x_s.at[GROUP, 1], x_r.at[GROUP, 1], other_core
    )

    def landed_wait(layer, slot, zz):
        ref = landed.at[layer, slot, zz]
        pltpu.make_async_copy(ref, ref, c_r.at[layer, slot, zz]).wait()

    def rotated(u):
        return (u * cosine[...] + pltpu.roll(u, HD // 2, 1) * sine[...]).astype(jnp.bfloat16)

    def product(step, core):
        return jnp.dot(
            scaled[core],
            wbuf[step % SLOTS, pl.ds(pl.multiple_of(core * HALF, HALF), HALF)],
            preferred_element_type=jnp.float32,
        )

    def finished(step, u):
        cols = pl.ds(pl.multiple_of(((step + 8) % CHUNKS) * CHUNK, CHUNK), CHUNK)
        scale = rows[...]
        for h in range(2):
            lanes = slice(h * HD, (h + 1) * HD)
            projected[step, :, lanes] = u[:, lanes] * scale + bias[:, cols][:, lanes]

    def first_half(step, carry):
        weight_copy(step).wait()
        projected[step] = product(step, t)
        return carry

    def second_half(step, carry):
        finished(step, projected[step] + product(step, 1 - t))

        @pl.when(step + SLOTS < CHUNKS)
        def _():
            weight_copy(step + SLOTS).start()

        return carry

    @pl.when(p == 0)
    def _():
        load_hidden.wait()

        def body(slot, carry):
            for zz in range(2):
                prepare(slot, zz, False)
            return carry

        lax.fori_loop(0, GROUP, body, 0)
        lax.fori_loop(0, EARLY, first_half, 0)

    pl.semaphore_wait(barrier, 2 * GROUP + 2)

    @pl.when(p == 0)
    def _():
        scaled_whole.start()
        squares_copy.start()

    for k in range(PIECES):
        weight_up(k).start()
        weight_down(k).start()
    for step in range(EARLY, SLOTS):
        weight_copy(step).start()
    for copy in own_weights:
        copy.start()

    @pl.when(p == 0)
    def _():
        for k in range(PIECES):
            send_across(hidden, k).start()

    @pl.when(p == 1)
    def _():
        for k in range(PIECES):
            weight_over(k).start()
        for k in range(PIECES):
            pass_weights(k)
            send_across(hidden, k).wait_recv()
            pass_across(x_in, k).start()
            weight_over(k).wait_recv()
            weight_on(k, 5).start()
            weight_on(k, 6).start()
        for k in range(PIECES):
            weight_pass_up(k).wait_recv()
            weight_pass_down(k).wait_recv()
            weight_opposite(k).start()
        for k in range(PIECES):
            pass_across(x_in, k).wait_recv()

        def body(j, carry):
            slot = (own + j) % GROUP
            for zz in range(2):
                landed_wait(0, slot, zz)
                prepare(slot, zz, True)
                scaled_copy(slot, zz).start()
            return carry

        lax.fori_loop(0, GROUP, body, 0)
        squares_copy.start()
        for k in range(PIECES):
            send_across(x_own, k).start()

    lax.fori_loop(EARLY * (1 - p), SLOTS, first_half, 0)
    squares_copy.wait_recv()

    @pl.when(p == 0)
    def _():
        scaled_whole.wait_recv()

    @pl.when(p == 1)
    def _():
        for slot in range(GROUP):
            for zz in range(2):
                scaled_copy(slot, zz).wait_recv()

    mean = jnp.sum(squares[0] + squares[1], axis=1, keepdims=True) * (1.0 / D)
    rows[...] = jnp.broadcast_to(lax.rsqrt(mean + EPSILON), (SEQ, SEQ))
    lax.fori_loop(0, 3, second_half, 0)
    for h in range(2):
        keys[h] = rotated(projected[0, :, h * HD : (h + 1) * HD])
        values[h] = projected[1, :, h * HD : (h + 1) * HD].astype(jnp.bfloat16)

    def attend(step):
        q_chunk = step - 2
        kv = q_chunk // 4
        for h in range(2):
            scores = lax.dot_general(
                rotated(projected[step, :, h * HD : (h + 1) * HD]),
                keys[kv],
                (((1,), (1,)), ((), ())),
                preferred_element_type=jnp.float32,
            ) * (1.0 / math.sqrt(HD))
            exponent = jnp.where(mask[...] > 0.0, jnp.exp(scores), 0.0)
            weight = exponent * (1.0 / jnp.sum(exponent, axis=1, keepdims=True))
            attended = jnp.dot(
                weight.astype(jnp.bfloat16), values[kv], preferred_element_type=jnp.float32
            )
            cols = pl.multiple_of((q_chunk % 2) * CHUNK + h * HD, HD)
            gathered[q_chunk // 2, own, :, pl.ds(cols, HD)] = attended.astype(jnp.bfloat16)

    def pass_on(q_chunk):
        @pl.when(q_chunk % 2 == 1)
        def _():
            inject(q_chunk // 2)

    def project_second(step, carry):
        attend(step - 1)
        finished(step, projected[step] + product(step, 1 - t))
        pass_on(step - 3)
        return carry

    def project_both(step, carry):
        weight_copy(step).wait()
        attend(step - 1)
        finished(step, product(step, 0) + product(step, 1))
        pass_on(step - 3)
        return carry

    lax.fori_loop(3, SLOTS, project_second, 0)
    lax.fori_loop(SLOTS, CHUNKS, project_both, 0)
    attend(CHUNKS - 1)
    inject(PIECES - 1)

    def stream_of(e):
        return e + p * (xl - e % 2)

    def place_of(e):
        return own + p * (e % 2 - xl)

    def part_copy(e, zz):
        return copy_to(
            part_out.at[e, zz], part_in.at[e, zz], p_s.at[e, zz], p_r.at[e, zz], other_core
        )

    def sums_copy(e, zz):
        return copy_to(
            sums.at[e, zz],
            landed.at[p, place_of(e), zz],
            c_s.at[e, zz],
            c_r.at[p, place_of(e), zz],
            device(stream_of(e), pipe=1),
        )

    def nth(j):
        pair, odd = j // 2, j % 2
        along = (pair * (3 - pair)) // 2
        dy = along * (3 + 2 * odd) + 2 * (pair // 3)
        dx = (1 - along) * odd + (pair // 2) * (1 - pair // 3)
        return at(y + dy, (xl + dx) % 2)

    def unit(e, zb):
        stream, xb = stream_of(e), xl + p * (e % 2 - xl)
        part = jnp.dot(gathered[0, stream], weights[xb, zb, 0], preferred_element_type=jnp.float32)
        for k in range(1, PIECES):
            part += jnp.dot(
                gathered[k, stream], weights[xb, zb, k], preferred_element_type=jnp.float32
            )

        @pl.when(zb // 2 == t)
        def _():
            total[e, zb % 2] = part

        @pl.when(zb // 2 != t)
        def _():
            part_out[e, zb % 2] = part.astype(jnp.bfloat16)
            part_copy(e, zb % 2).start()

    def finish(e, zb):
        zz = zb % 2

        @pl.when(zb // 2 == t)
        def _():
            part_copy(e, zz).wait_recv()
            sums[e, zz] = (total[e, zz] + part_in[e, zz].astype(jnp.float32)).astype(jnp.bfloat16)

            @pl.when((p == 0) | (e // 2 != y))
            def _():
                sums_copy(e, zz).start()

    def each(action, count, place):
        def body(i, carry):
            j, turn = place(i)
            action(nth(j), (z + turn) % 4)
            return carry

        lax.fori_loop(0, count, body, 0)

    def each_along(action, dy):
        def body(i, carry):
            action(at(y + dy, (xl + i // 4) % 2), (z + i % 4) % 4)
            return carry

        lax.fori_loop(0, 8, body, 0)

    def near(i):
        return i, 0

    def beside(i):
        return i // 2, 1 + 2 * (i % 2)

    def corner(i):
        return 4 + i // 3, i % 3 + (i % 3) // 2

    def facing(i):
        return 6, i + i // 2

    def far(i):
        return i, 2

    def last(i):
        return 7, i

    for copy in own_weights:
        copy.wait()

    @pl.when(p == 0)
    def _():
        pass_first(0)
        pass_weights(0)
        pass_first(1)
        pass_first(2)
        pass_weights(1)
        pass_first(3)
        each(unit, 4, near)
        pass_weights(2)
        pass_second(0)
        each(finish, 4, near)
        pass_second(1)
        pass_weights(3)
        each(unit, 8, beside)
        pass_second(2)
        each(finish, 8, beside)
        pass_second(3)
        for k in range(PIECES):
            rows_copy(k, 3).wait_recv()
            rows_copy(k, 4).wait_recv()
        each(unit, 6, corner)
        each(finish, 6, corner)
        each(unit, 3, facing)
        each(finish, 3, facing)
        for k in range(PIECES):
            weight_pass_up(k).wait_recv()
            weight_pass_down(k).wait_recv()
        each(unit, 7, far)
        each(finish, 7, far)
        for k in range(PIECES):
            rows_copy(k, 7).wait_recv()
        each(unit, 4, last)
        each(finish, 4, last)

    @pl.when(p == 1)
    def _():
        for k in range(PIECES):
            pass_along(k)
        for k in range(PIECES):
            weight_on(k, 5).wait_recv()
            weight_on(k, 6).wait_recv()
            weight_opposite(k).wait_recv()
        each_along(unit, 3)
        each_along(finish, 3)
        each_along(unit, 1)
        each_along(finish, 1)
        each_along(unit, 0)
        for k in range(PIECES):
            rows_copy(k, 5).wait_recv()
            rows_copy(k, 6).wait_recv()
        each_along(unit, 2)
        each_along(finish, 2)
        each_along(finish, 0)

    @pl.when(p == 0)
    def _():
        for k in range(PIECES):
            send_across(x_own, k).wait_recv()
            pass_across(out, k).start()
        for e in range(GROUP):
            for zz in range(2):
                sums_copy(e, zz).wait_send()
        for k in range(PIECES):
            send_across(hidden, k).wait_send()
            pass_across(out, k).wait()
            for kind in (0, 3, 4, 7):
                rows_copy(k, kind).wait_send()
        scaled_whole.wait_send()

    @pl.when(p == 1)
    def _():
        def add(slot, zz, update):
            cols = block(slot, zz)
            out[:, cols] = (
                x_own[:, cols].astype(jnp.float32) + update.astype(jnp.float32)
            ).astype(jnp.bfloat16)

        def body(i, carry):
            slot = at(y + 1 + i // 2, i % 2)
            for zz in range(2):
                landed_wait(1, slot, zz)
                add(slot, zz, landed[1, slot, zz])
            return carry

        for xb in range(2):
            for zz in range(2):
                add(at(y, xb), zz, sums[at(y, xb), zz])
        lax.fori_loop(0, GROUP - 2, body, 0)
        for j in range(2, GROUP):
            for zz in range(2):
                sums_copy((2 * y + j) % GROUP, zz).wait_send()
        for k in range(PIECES):
            send_across(x_own, k).wait_send()
            pass_across(x_in, k).wait_send()
            weight_over(k).wait_send()
            weight_on(k, 5).wait_send()
            weight_on(k, 6).wait_send()
            weight_opposite(k).wait_send()
        for slot in range(GROUP):
            for zz in range(2):
                scaled_copy(slot, zz).wait_send()

    for k in range(PIECES):
        for copy in (weight_up(k), weight_down(k), weight_pass_up(k), weight_pass_down(k)):
            copy.wait_send()
        for kind in (1, 2, 5, 6):
            rows_copy(k, kind).wait_send()
    squares_copy.wait_send()
    for e in range(GROUP):
        for zz in range(2):
            part_copy(e, zz).wait_send()


def local(hidden, gain, qkv, bias, out_weight, segment, start, height, width, count):
    bf16, f32 = jnp.bfloat16, jnp.float32
    anywhere = pl.BlockSpec(memory_space=pl.ANY)
    vmem = pl.BlockSpec(memory_space=pltpu.VMEM)
    smem = pl.BlockSpec(memory_space=pltpu.SMEM)
    dma = pltpu.SemaphoreType.DMA
    result = pl.pallas_call(
        kernel,
        out_shape=jax.ShapeDtypeStruct((SEQ, HALF), bf16),
        in_specs=[anywhere, vmem, anywhere, vmem, anywhere, vmem, smem, smem, smem, smem],
        out_specs=vmem,
        scratch_shapes=[
            pltpu.VMEM((SLOTS, D, CHUNK), bf16),
            pltpu.VMEM((PIECES, GROUP, SEQ, PIECE), bf16),
            pltpu.VMEM((2, 4, PIECES, PIECE, BLOCK), bf16),
            pltpu.VMEM((2, SEQ, HALF), bf16),
            pltpu.VMEM((2, SEQ, 128), f32),
            pltpu.VMEM((SEQ, HALF), bf16),
            pltpu.VMEM((SEQ, HALF), bf16),
            pltpu.VMEM((SEQ, HALF), bf16),
            pltpu.VMEM((GROUP, 2, SEQ, BLOCK), f32),
            pltpu.VMEM((GROUP, 2, SEQ, BLOCK), bf16),
            pltpu.VMEM((GROUP, 2, SEQ, BLOCK), bf16),
            pltpu.VMEM((GROUP, 2, SEQ, BLOCK), bf16),
            pltpu.VMEM((2, GROUP, 2, SEQ, BLOCK), bf16),
            pltpu.VMEM((CHUNKS, SEQ, CHUNK), f32),
            pltpu.VMEM((SEQ, SEQ), f32),
            pltpu.VMEM((SEQ, SEQ), f32),
            pltpu.VMEM((SEQ, SEQ), f32),
            pltpu.VMEM((SEQ, SEQ), f32),
            pltpu.VMEM((2, SEQ, HD), bf16),
            pltpu.VMEM((2, SEQ, HD), bf16),
            dma((SLOTS,)),
            dma((PIECES + 1,)),
            dma((8, PIECES)),
            dma((8, PIECES)),
            dma((8, PIECES)),
            dma((8, PIECES)),
            dma((GROUP + 1, 2)),
            dma((GROUP + 1, 2)),
            dma((GROUP, 2)),
            dma((GROUP, 2)),
            dma((GROUP, 2)),
            dma((2, GROUP, 2)),
            dma((PIECES,)),
            dma((PIECES,)),
            dma((PIECES,)),
            dma((PIECES,)),
        ],
        compiler_params=pltpu.CompilerParams(
            collective_id=0, has_side_effects=True, vmem_limit_bytes=61 * MIB
        ),
        name="sublayers",
    )(
        hidden[0],
        gain,
        qkv[0],
        bias,
        out_weight[0],
        segment,
        start,
        height,
        width,
        count,
    )
    return result[None, None]


def solution(mesh):
    return jax.shard_map(
        local,
        mesh=mesh,
        in_specs=(
            P(None, "dp", "tensor"),
            P("pipe", None),
            P("pipe", None, "tensor"),
            P("pipe", "tensor"),
            P("pipe", "tensor", "dp"),
            P(None, "dp"),
            P(None, "dp"),
            P(None, "dp"),
            P(None, "dp"),
            P(None, "dp"),
        ),
        out_specs=P("pipe", None, "dp", "tensor"),
        check_vma=False,
    )
```

```python
import math

import jax
import jax.numpy as jnp
from jax import lax
from jax.experimental import pallas as pl
from jax.experimental.pallas import tpu as pltpu
from jax.sharding import PartitionSpec as P

HD = 128
SEQ = 128
D = 8192
HALF = 4096
QUERY = 2048
CHUNK = 256
CHUNKS = 10
SLOTS = 8
EARLY = 1
AHEAD = 2
PIECES = 4
PIECE = 512
GROUP = 8
BLOCK = 256
THETA = 1000000.0
EPSILON = 1e-06
MIB = 1 << 20
MESH = pl.DeviceIdType.MESH


def copy_to(src, dst, send, recv, device):
    return pltpu.make_async_remote_copy(
        src_ref=src,
        dst_ref=dst,
        send_sem=send,
        recv_sem=recv,
        device_id=device,
        device_id_type=MESH,
    )


def rotary_tables(seg_ref, start_ref, height_ref, width_ref, count_ref):
    row = lax.broadcasted_iota(jnp.int32, (SEQ, SEQ), 0)
    lane = lax.broadcasted_iota(jnp.int32, (SEQ, SEQ), 1)
    seg_keys = jnp.broadcast_to(seg_ref[...].astype(jnp.float32), (SEQ, SEQ))
    seg = jnp.sum(jnp.where(row == lane, seg_keys, 0.0), axis=1, keepdims=True)
    seg = jnp.broadcast_to(seg, (SEQ, SEQ))
    allowed = (row >= lane) & (seg == seg_keys)
    border = jnp.sum(jnp.where(seg_keys == 0.0, 1.0, 0.0), axis=1, keepdims=True)
    first = seg == 0.0

    def choose(ref):
        return jnp.where(
            first, ref[0, 0].astype(jnp.float32), ref[0, 1].astype(jnp.float32)
        )

    begin = jnp.where(first, 0.0, border)
    anchor = choose(start_ref)
    tall = choose(height_ref)
    broad = choose(width_ref)
    present = choose(count_ref)
    counter = row.astype(jnp.float32)
    span = tall * broad * present
    offset = counter - anchor
    inside = (offset >= 0.0) & (offset < span)
    relative = counter - begin
    shifted = relative - span + present * jnp.maximum(tall, broad)
    text = jnp.where(offset >= span, shifted, relative)
    base = anchor - begin
    clipped = jnp.maximum(offset, 0.0)
    grid_row = jnp.floor((clipped + 0.5) / broad)
    grid_col = clipped - grid_row * broad
    freq = lane % (HD // 2)
    inverse = jnp.exp(freq.astype(jnp.float32) * (-2.0 * math.log(THETA) / HD))
    moved = jnp.where(
        freq < HD // 8, 0.0, jnp.where(freq < HD // 8 + 3 * HD // 16, grid_row, grid_col)
    )
    angles = jnp.where(inside, base + moved, text) * inverse
    sine = jnp.sin(angles)
    return jnp.cos(angles), jnp.where(lane < HD // 2, -sine, sine), allowed


def kernel(
    hidden,
    gain_in,
    qkv,
    bias_in,
    out_weight,
    seg_in,
    start_in,
    height_in,
    width_in,
    count_in,
    out,
    gain,
    bias,
    seg,
    start,
    height,
    width,
    count,
    small_sem,
    wbuf,
    gathered,
    weights,
    scaled,
    squares,
    x_own,
    x_in,
    x_relay,
    total,
    part_out,
    part_in,
    sums,
    landed,
    projected,
    cosine,
    sine,
    mask,
    rows,
    keys,
    values,
    w_sem,
    local_sem,
    ws,
    wr,
    a_s,
    a_r,
    x_s,
    x_r,
    p_s,
    p_r,
    c_s,
    c_r,
    r_s,
    r_r,
    f_s,
    f_r,
):
    p = lax.axis_index("pipe")
    d = lax.axis_index("dp")
    t = lax.axis_index("tensor")
    xl = d % 2
    y = (d // 2) % 4
    z = d // 8

    def at(y_, xl_):
        return (y_ % 4) * 2 + xl_

    def device(slot, pipe=p, z_=z):
        return (pipe, (z_ % 4) * 8 + slot, t)

    own = at(y, xl)
    other_core = (p, d, 1 - t)
    partner = device(at(y, 1 - xl))
    y_up, y_down = device(at(y + 1, xl)), device(at(y + 3, xl))
    z_up, z_down = device(own, z_=z + 1), device(own, z_=z + 3)
    across = device(at(y, 1 - xl), pipe=1 - p)

    def weight_copy(step):
        chunk = (step + 8) % CHUNKS
        slot = step % SLOTS
        return pltpu.make_async_copy(
            qkv.at[:, pl.ds(pl.multiple_of(chunk * CHUNK, CHUNK), CHUNK)],
            wbuf.at[slot],
            w_sem.at[slot],
        )

    load_hidden = pltpu.make_async_copy(hidden, x_in, local_sem.at[PIECES])
    small = [
        pltpu.make_async_copy(src, dst, small_sem.at[i])
        for i, (src, dst) in enumerate(
            (
                (seg_in, seg),
                (start_in, start),
                (height_in, height),
                (width_in, width),
                (count_in, count),
                (gain_in, gain),
                (bias_in, bias),
            )
        )
    ]
    for copy in small:
        copy.start()

    @pl.when(p == 0)
    def _():
        load_hidden.start()

    for step in range(AHEAD):
        weight_copy(step).start()
    own_weights = [
        pltpu.make_async_copy(
            out_weight.at[pl.ds(k * PIECE, PIECE)], weights.at[xl, z, k], local_sem.at[k]
        )
        for k in range(PIECES)
    ]

    barrier = pltpu.get_barrier_semaphore()
    pl.semaphore_signal(barrier, inc=1, device_id=other_core, device_id_type=MESH)
    for to in (z_up, z_down):
        pl.semaphore_signal(barrier, inc=1, device_id=to, device_id_type=MESH)
    for j in range(GROUP):
        slot = (own + j) % GROUP
        pl.semaphore_signal(
            barrier, inc=1, device_id=device(slot, pipe=1 - p), device_id_type=MESH
        )
        if j:
            pl.semaphore_signal(barrier, inc=1, device_id=device(slot), device_id_type=MESH)

    def weight_up(k):
        src = out_weight.at[pl.ds(k * PIECE, PIECE)]
        return copy_to(src, weights.at[xl, z, k], ws.at[0, k], wr.at[0, k], z_up)

    def weight_down(k):
        src = out_weight.at[pl.ds(k * PIECE, PIECE)]
        return copy_to(src, weights.at[xl, z, k], ws.at[1, k], wr.at[1, k], z_down)

    def weight_pass_up(k):
        ref = weights.at[xl, (z + 3) % 4, k, pl.ds(0, PIECE // 2)]
        return copy_to(ref, ref, ws.at[2, k], wr.at[2, k], z_up)

    def weight_pass_down(k):
        ref = weights.at[xl, (z + 1) % 4, k, pl.ds(PIECE // 2, PIECE // 2)]
        return copy_to(ref, ref, ws.at[3, k], wr.at[3, k], z_down)

    def weight_over(k):
        src = out_weight.at[pl.ds(k * PIECE, PIECE)]
        return copy_to(src, weights.at[xl, z, k], ws.at[4, k], wr.at[4, k], partner)

    def weight_on(k, kind):
        ref = weights.at[1 - xl, z, k]
        return copy_to(ref, ref, ws.at[kind, k], wr.at[kind, k], z_up if kind == 5 else z_down)

    def weight_opposite(k):
        ref = weights.at[xl, (z + 2) % 4, k]
        return copy_to(ref, ref, ws.at[7, k], wr.at[7, k], partner)

    def pass_weights(k):
        weight_up(k).wait_recv()
        weight_pass_up(k).start()
        weight_down(k).wait_recv()
        weight_pass_down(k).start()

    half = SEQ // 2

    def rows_copy(k, kind):
        ref, to = {
            0: (gathered.at[k, own], partner),
            1: (gathered.at[k, own], y_up),
            2: (gathered.at[k, own], y_down),
            3: (gathered.at[k, at(y, 1 - xl)], y_up),
            4: (gathered.at[k, at(y, 1 - xl)], y_down),
            5: (gathered.at[k, at(y + 3, xl), pl.ds(0, half)], y_up),
            6: (gathered.at[k, at(y + 1, xl), pl.ds(half, half)], y_down),
            7: (gathered.at[k, at(y + 2, xl)], partner),
        }[kind]
        return copy_to(ref, ref, a_s.at[kind, k], a_r.at[kind, k], to)

    def inject(k):
        for kind in (1, 2):
            rows_copy(k, kind).start()

        @pl.when(p == 0)
        def _():
            rows_copy(k, 0).start()

    def pass_first(k):
        rows_copy(k, 0).wait_recv()
        rows_copy(k, 3).start()
        rows_copy(k, 4).start()
        pass_along(k)

    def pass_along(k):
        rows_copy(k, 1).wait_recv()
        rows_copy(k, 5).start()
        rows_copy(k, 2).wait_recv()
        rows_copy(k, 6).start()

    def pass_second(k):
        rows_copy(k, 5).wait_recv()
        rows_copy(k, 6).wait_recv()
        rows_copy(k, 7).start()

    def strip(k):
        return pl.ds(k * (SEQ // PIECES), SEQ // PIECES)

    def send_across(src, k):
        return copy_to(src.at[strip(k)], x_relay.at[strip(k)], r_s.at[k], r_r.at[k], across)

    def pass_across(dst, k):
        return copy_to(x_relay.at[strip(k)], dst.at[strip(k)], f_s.at[k], f_r.at[k], partner)

    for copy in small:
        copy.wait()
    cos, sin, allowed = rotary_tables(seg, start, height, width, count)
    cosine[...] = cos
    sine[...] = sin
    mask[...] = jnp.where(allowed, 1.0, 0.0)
    squares[t] = jnp.zeros((SEQ, 128), jnp.float32)

    def block(slot, zz):
        return pl.ds(pl.multiple_of(zz * 2048 + slot * BLOCK, BLOCK), BLOCK)

    def prepare(slot, zz, update):
        cols = block(slot, zz)
        x = x_in[:, cols]
        if update:
            x = x.astype(jnp.float32) + landed[0, slot, zz].astype(jnp.float32)
            x = x.astype(jnp.bfloat16)
        x_own[:, cols] = x
        x = x.astype(jnp.float32)
        g = gain[:, pl.ds(pl.multiple_of(t * HALF + zz * 2048 + slot * BLOCK, BLOCK), BLOCK)]
        scaled[t, :, cols] = (x * g).astype(jnp.bfloat16)
        x = x * x
        squares[t] += x[:, 0:128] + x[:, 128:256]

    def scaled_copy(slot, zz):
        ref = scaled.at[t, :, block(slot, zz)]
        return copy_to(ref, ref, x_s.at[slot, zz], x_r.at[slot, zz], other_core)

    squares_copy = copy_to(
        squares.at[t], squares.at[t], x_s.at[GROUP, 0], x_r.at[GROUP, 0], other_core
    )
    scaled_whole = copy_to(
        scaled.at[t], scaled.at[t], x_s.at[GROUP, 1], x_r.at[GROUP, 1], other_core
    )

    def landed_wait(layer, slot, zz):
        ref = landed.at[layer, slot, zz]
        pltpu.make_async_copy(ref, ref, c_r.at[layer, slot, zz]).wait()

    def rotated(u):
        return (u * cosine[...] + pltpu.roll(u, HD // 2, 1) * sine[...]).astype(jnp.bfloat16)

    def product(step, core):
        return jnp.dot(
            scaled[core],
            wbuf[step % SLOTS, pl.ds(pl.multiple_of(core * HALF, HALF), HALF)],
            preferred_element_type=jnp.float32,
        )

    def finished(step, u):
        cols = pl.ds(pl.multiple_of(((step + 8) % CHUNKS) * CHUNK, CHUNK), CHUNK)
        scale = rows[...]
        for h in range(2):
            lanes = slice(h * HD, (h + 1) * HD)
            projected[step, :, lanes] = u[:, lanes] * scale + bias[:, cols][:, lanes]

    def first_half(step, carry):
        weight_copy(step).wait()
        projected[step] = product(step, t)
        return carry

    def second_half(step, carry):
        finished(step, projected[step] + product(step, 1 - t))

        @pl.when(step + SLOTS < CHUNKS)
        def _():
            weight_copy(step + SLOTS).start()

        return carry

    @pl.when(p == 0)
    def _():
        load_hidden.wait()

        def body(slot, carry):
            for zz in range(2):
                prepare(slot, zz, False)
            return carry

        lax.fori_loop(0, GROUP, body, 0)
        lax.fori_loop(0, EARLY, first_half, 0)

    pl.semaphore_wait(barrier, 2 * GROUP + 2)

    @pl.when(p == 0)
    def _():
        scaled_whole.start()
        squares_copy.start()

    for step in range(AHEAD, SLOTS):
        weight_copy(step).start()
    for k in range(PIECES):
        weight_up(k).start()
        weight_down(k).start()
    for copy in own_weights:
        copy.start()

    @pl.when(p == 0)
    def _():
        for k in range(PIECES):
            send_across(hidden, k).start()

    @pl.when(p == 1)
    def _():
        for k in range(PIECES):
            weight_over(k).start()
        for k in range(PIECES):
            pass_weights(k)
            send_across(hidden, k).wait_recv()
            pass_across(x_in, k).start()
            weight_over(k).wait_recv()
            weight_on(k, 5).start()
            weight_on(k, 6).start()
        for k in range(PIECES):
            weight_pass_up(k).wait_recv()
            weight_pass_down(k).wait_recv()
            weight_opposite(k).start()
        for k in range(PIECES):
            pass_across(x_in, k).wait_recv()

        def body(j, carry):
            slot = (own + j) % GROUP
            for zz in range(2):
                landed_wait(0, slot, zz)
                prepare(slot, zz, True)
                scaled_copy(slot, zz).start()
            return carry

        lax.fori_loop(0, GROUP, body, 0)
        squares_copy.start()
        for k in range(PIECES):
            send_across(x_own, k).start()

    lax.fori_loop(EARLY * (1 - p), SLOTS, first_half, 0)
    squares_copy.wait_recv()

    @pl.when(p == 0)
    def _():
        scaled_whole.wait_recv()

    @pl.when(p == 1)
    def _():
        for slot in range(GROUP):
            for zz in range(2):
                scaled_copy(slot, zz).wait_recv()

    mean = jnp.sum(squares[0] + squares[1], axis=1, keepdims=True) * (1.0 / D)
    rows[...] = jnp.broadcast_to(lax.rsqrt(mean + EPSILON), (SEQ, SEQ))
    lax.fori_loop(0, 3, second_half, 0)
    for h in range(2):
        keys[h] = rotated(projected[0, :, h * HD : (h + 1) * HD])
        values[h] = projected[1, :, h * HD : (h + 1) * HD].astype(jnp.bfloat16)

    def attend(step):
        q_chunk = step - 2
        kv = q_chunk // 4
        for h in range(2):
            scores = lax.dot_general(
                rotated(projected[step, :, h * HD : (h + 1) * HD]),
                keys[kv],
                (((1,), (1,)), ((), ())),
                preferred_element_type=jnp.float32,
            ) * (1.0 / math.sqrt(HD))
            exponent = jnp.where(mask[...] > 0.0, jnp.exp(scores), 0.0)
            weight = exponent * (1.0 / jnp.sum(exponent, axis=1, keepdims=True))
            attended = jnp.dot(
                weight.astype(jnp.bfloat16), values[kv], preferred_element_type=jnp.float32
            )
            cols = pl.multiple_of((q_chunk % 2) * CHUNK + h * HD, HD)
            gathered[q_chunk // 2, own, :, pl.ds(cols, HD)] = attended.astype(jnp.bfloat16)

    def pass_on(q_chunk):
        @pl.when(q_chunk % 2 == 1)
        def _():
            inject(q_chunk // 2)

    def project_second(step, carry):
        attend(step - 1)
        finished(step, projected[step] + product(step, 1 - t))
        pass_on(step - 3)
        return carry

    def project_both(step, carry):
        weight_copy(step).wait()
        attend(step - 1)
        finished(step, product(step, 0) + product(step, 1))
        pass_on(step - 3)
        return carry

    lax.fori_loop(3, SLOTS, project_second, 0)
    lax.fori_loop(SLOTS, CHUNKS, project_both, 0)
    attend(CHUNKS - 1)
    inject(PIECES - 1)

    def stream_of(e):
        return e + p * (xl - e % 2)

    def place_of(e):
        return own + p * (e % 2 - xl)

    def part_copy(e, zz):
        return copy_to(
            part_out.at[e, zz], part_in.at[e, zz], p_s.at[e, zz], p_r.at[e, zz], other_core
        )

    def sums_copy(e, zz):
        return copy_to(
            sums.at[e, zz],
            landed.at[p, place_of(e), zz],
            c_s.at[e, zz],
            c_r.at[p, place_of(e), zz],
            device(stream_of(e), pipe=1),
        )

    def nth(j):
        pair, odd = j // 2, j % 2
        along = (pair * (3 - pair)) // 2
        dy = along * (3 + 2 * odd) + 2 * (pair // 3)
        dx = (1 - along) * odd + (pair // 2) * (1 - pair // 3)
        return at(y + dy, (xl + dx) % 2)

    def unit(e, zb):
        stream, xb = stream_of(e), xl + p * (e % 2 - xl)
        part = jnp.dot(gathered[0, stream], weights[xb, zb, 0], preferred_element_type=jnp.float32)
        for k in range(1, PIECES):
            part += jnp.dot(
                gathered[k, stream], weights[xb, zb, k], preferred_element_type=jnp.float32
            )

        @pl.when(zb // 2 == t)
        def _():
            total[e, zb % 2] = part

        @pl.when(zb // 2 != t)
        def _():
            part_out[e, zb % 2] = part.astype(jnp.bfloat16)
            part_copy(e, zb % 2).start()

    def finish(e, zb):
        zz = zb % 2

        @pl.when(zb // 2 == t)
        def _():
            part_copy(e, zz).wait_recv()
            sums[e, zz] = (total[e, zz] + part_in[e, zz].astype(jnp.float32)).astype(jnp.bfloat16)

            @pl.when((p == 0) | (e // 2 != y))
            def _():
                sums_copy(e, zz).start()

    def each(action, count, place):
        def body(i, carry):
            j, turn = place(i)
            action(nth(j), (z + turn) % 4)
            return carry

        lax.fori_loop(0, count, body, 0)

    def each_along(action, dy):
        def body(i, carry):
            action(at(y + dy, (xl + i // 4) % 2), (z + i % 4) % 4)
            return carry

        lax.fori_loop(0, 8, body, 0)

    def near(i):
        return i, 0

    def beside(i):
        return i // 2, 1 + 2 * (i % 2)

    def corner(i):
        return 4 + i // 4, i % 4

    def facing(i):
        return 6, i

    def far(i):
        return i, 2

    def last(i):
        return 7, i

    for copy in own_weights:
        copy.wait()

    @pl.when(p == 0)
    def _():
        pass_first(0)
        pass_weights(0)
        pass_first(1)
        pass_first(2)
        pass_weights(1)
        pass_first(3)
        pass_weights(2)
        each(unit, 4, near)
        pass_weights(3)
        each(finish, 4, near)
        each(unit, 8, beside)
        pass_second(0)
        each(finish, 8, beside)
        pass_second(1)
        for k in range(PIECES):
            weight_pass_up(k).wait_recv()
            weight_pass_down(k).wait_recv()
        each(unit, 4, far)
        each(finish, 4, far)
        pass_second(2)
        pass_second(3)
        for k in range(PIECES):
            rows_copy(k, 3).wait_recv()
            rows_copy(k, 4).wait_recv()
        each(unit, 8, corner)
        each(finish, 8, corner)
        each(unit, 4, facing)
        each(finish, 4, facing)
        for k in range(PIECES):
            rows_copy(k, 7).wait_recv()
        each(unit, 4, last)
        each(finish, 4, last)

    @pl.when(p == 1)
    def _():
        pass_along(0)
        pass_along(1)
        for k in range(PIECES):
            weight_on(k, 5).wait_recv()
            weight_on(k, 6).wait_recv()
            weight_opposite(k).wait_recv()
        each_along(unit, 0)
        pass_along(2)
        pass_along(3)
        each_along(unit, 3)
        each_along(finish, 3)
        each_along(unit, 1)
        each_along(finish, 1)
        for k in range(PIECES):
            rows_copy(k, 5).wait_recv()
            rows_copy(k, 6).wait_recv()
        each_along(unit, 2)
        each_along(finish, 2)
        each_along(finish, 0)

    @pl.when(p == 0)
    def _():
        for k in range(PIECES):
            send_across(x_own, k).wait_recv()
            pass_across(out, k).start()
        for e in range(GROUP):
            for zz in range(2):
                sums_copy(e, zz).wait_send()
        for k in range(PIECES):
            send_across(hidden, k).wait_send()
            pass_across(out, k).wait()
            for kind in (0, 3, 4, 7):
                rows_copy(k, kind).wait_send()
        scaled_whole.wait_send()

    @pl.when(p == 1)
    def _():
        def add(slot, zz, update):
            cols = block(slot, zz)
            out[:, cols] = (
                x_own[:, cols].astype(jnp.float32) + update.astype(jnp.float32)
            ).astype(jnp.bfloat16)

        def body(i, carry):
            slot = at(y + 1 + i // 2, i % 2)
            for zz in range(2):
                landed_wait(1, slot, zz)
                add(slot, zz, landed[1, slot, zz])
            return carry

        for xb in range(2):
            for zz in range(2):
                add(at(y, xb), zz, sums[at(y, xb), zz])
        lax.fori_loop(0, GROUP - 2, body, 0)
        for j in range(2, GROUP):
            for zz in range(2):
                sums_copy((2 * y + j) % GROUP, zz).wait_send()
        for k in range(PIECES):
            send_across(x_own, k).wait_send()
            pass_across(x_in, k).wait_send()
            weight_over(k).wait_send()
            weight_on(k, 5).wait_send()
            weight_on(k, 6).wait_send()
            weight_opposite(k).wait_send()
        for slot in range(GROUP):
            for zz in range(2):
                scaled_copy(slot, zz).wait_send()

    for k in range(PIECES):
        for copy in (weight_up(k), weight_down(k), weight_pass_up(k), weight_pass_down(k)):
            copy.wait_send()
        for kind in (1, 2, 5, 6):
            rows_copy(k, kind).wait_send()
    squares_copy.wait_send()
    for e in range(GROUP):
        for zz in range(2):
            part_copy(e, zz).wait_send()


def local(hidden, gain, qkv, bias, out_weight, segment, start, height, width, count):
    bf16, f32 = jnp.bfloat16, jnp.float32
    anywhere = pl.BlockSpec(memory_space=pl.ANY)
    vmem = pl.BlockSpec(memory_space=pltpu.VMEM)
    dma = pltpu.SemaphoreType.DMA
    result = pl.pallas_call(
        kernel,
        out_shape=jax.ShapeDtypeStruct((SEQ, HALF), bf16),
        in_specs=[anywhere] * 10,
        out_specs=vmem,
        scratch_shapes=[
            pltpu.VMEM(gain.shape, f32),
            pltpu.VMEM(bias.shape, f32),
            pltpu.VMEM(segment.shape, jnp.int32),
            pltpu.SMEM(start.shape, jnp.int32),
            pltpu.SMEM(height.shape, jnp.int32),
            pltpu.SMEM(width.shape, jnp.int32),
            pltpu.SMEM(count.shape, jnp.int32),
            dma((7,)),
            pltpu.VMEM((SLOTS, D, CHUNK), bf16),
            pltpu.VMEM((PIECES, GROUP, SEQ, PIECE), bf16),
            pltpu.VMEM((2, 4, PIECES, PIECE, BLOCK), bf16),
            pltpu.VMEM((2, SEQ, HALF), bf16),
            pltpu.VMEM((2, SEQ, 128), f32),
            pltpu.VMEM((SEQ, HALF), bf16),
            pltpu.VMEM((SEQ, HALF), bf16),
            pltpu.VMEM((SEQ, HALF), bf16),
            pltpu.VMEM((GROUP, 2, SEQ, BLOCK), f32),
            pltpu.VMEM((GROUP, 2, SEQ, BLOCK), bf16),
            pltpu.VMEM((GROUP, 2, SEQ, BLOCK), bf16),
            pltpu.VMEM((GROUP, 2, SEQ, BLOCK), bf16),
            pltpu.VMEM((2, GROUP, 2, SEQ, BLOCK), bf16),
            pltpu.VMEM((CHUNKS, SEQ, CHUNK), f32),
            pltpu.VMEM((SEQ, SEQ), f32),
            pltpu.VMEM((SEQ, SEQ), f32),
            pltpu.VMEM((SEQ, SEQ), f32),
            pltpu.VMEM((SEQ, SEQ), f32),
            pltpu.VMEM((2, SEQ, HD), bf16),
            pltpu.VMEM((2, SEQ, HD), bf16),
            dma((SLOTS,)),
            dma((PIECES + 1,)),
            dma((8, PIECES)),
            dma((8, PIECES)),
            dma((8, PIECES)),
            dma((8, PIECES)),
            dma((GROUP + 1, 2)),
            dma((GROUP + 1, 2)),
            dma((GROUP, 2)),
            dma((GROUP, 2)),
            dma((GROUP, 2)),
            dma((2, GROUP, 2)),
            dma((PIECES,)),
            dma((PIECES,)),
            dma((PIECES,)),
            dma((PIECES,)),
        ],
        compiler_params=pltpu.CompilerParams(
            collective_id=0, has_side_effects=True, vmem_limit_bytes=61 * MIB
        ),
        name="sublayers",
    )(
        hidden[0],
        gain,
        qkv[0],
        bias,
        out_weight[0],
        segment,
        start,
        height,
        width,
        count,
    )
    return result[None, None]


def solution(mesh):
    return jax.shard_map(
        local,
        mesh=mesh,
        in_specs=(
            P(None, "dp", "tensor"),
            P("pipe", None),
            P("pipe", None, "tensor"),
            P("pipe", "tensor"),
            P("pipe", "tensor", "dp"),
            P(None, "dp"),
            P(None, "dp"),
            P(None, "dp"),
            P(None, "dp"),
            P(None, "dp"),
        ),
        out_specs=P("pipe", None, "dp", "tensor"),
        check_vma=False,
    )
```

```python
import math

import jax
import jax.numpy as jnp
from jax import lax
from jax.experimental import pallas as pl
from jax.experimental.pallas import tpu as pltpu
from jax.sharding import PartitionSpec as P

HD = 128
SEQ = 128
D = 8192
HALF = 4096
QUERY = 2048
CHUNK = 256
CHUNKS = 10
SLOTS = 8
EARLY = 1
AHEAD = 2
PIECES = 4
PIECE = 512
GROUP = 8
BLOCK = 256
THETA = 1000000.0
EPSILON = 1e-06
MIB = 1 << 20
MESH = pl.DeviceIdType.MESH


def copy_to(src, dst, send, recv, device):
    return pltpu.make_async_remote_copy(
        src_ref=src,
        dst_ref=dst,
        send_sem=send,
        recv_sem=recv,
        device_id=device,
        device_id_type=MESH,
    )


def rotary_tables(seg_ref, start_ref, height_ref, width_ref, count_ref):
    row = lax.broadcasted_iota(jnp.int32, (SEQ, SEQ), 0)
    lane = lax.broadcasted_iota(jnp.int32, (SEQ, SEQ), 1)
    seg_keys = jnp.broadcast_to(seg_ref[...].astype(jnp.float32), (SEQ, SEQ))
    seg = jnp.sum(jnp.where(row == lane, seg_keys, 0.0), axis=1, keepdims=True)
    seg = jnp.broadcast_to(seg, (SEQ, SEQ))
    allowed = (row >= lane) & (seg == seg_keys)
    border = jnp.sum(jnp.where(seg_keys == 0.0, 1.0, 0.0), axis=1, keepdims=True)
    first = seg == 0.0

    def choose(ref):
        return jnp.where(
            first, ref[0, 0].astype(jnp.float32), ref[0, 1].astype(jnp.float32)
        )

    begin = jnp.where(first, 0.0, border)
    anchor = choose(start_ref)
    tall = choose(height_ref)
    broad = choose(width_ref)
    present = choose(count_ref)
    counter = row.astype(jnp.float32)
    span = tall * broad * present
    offset = counter - anchor
    inside = (offset >= 0.0) & (offset < span)
    relative = counter - begin
    shifted = relative - span + present * jnp.maximum(tall, broad)
    text = jnp.where(offset >= span, shifted, relative)
    base = anchor - begin
    clipped = jnp.maximum(offset, 0.0)
    grid_row = jnp.floor((clipped + 0.5) / broad)
    grid_col = clipped - grid_row * broad
    freq = lane % (HD // 2)
    inverse = jnp.exp(freq.astype(jnp.float32) * (-2.0 * math.log(THETA) / HD))
    moved = jnp.where(
        freq < HD // 8, 0.0, jnp.where(freq < HD // 8 + 3 * HD // 16, grid_row, grid_col)
    )
    angles = jnp.where(inside, base + moved, text) * inverse
    sine = jnp.sin(angles)
    return jnp.cos(angles), jnp.where(lane < HD // 2, -sine, sine), allowed


def kernel(
    hidden,
    gain_in,
    qkv,
    bias_in,
    out_weight,
    seg_in,
    start_in,
    height_in,
    width_in,
    count_in,
    out,
    gain,
    bias,
    seg,
    start,
    height,
    width,
    count,
    small_sem,
    wbuf,
    gathered,
    weights,
    scaled,
    squares,
    x_own,
    x_in,
    x_relay,
    total,
    part_out,
    part_in,
    sums,
    landed,
    projected,
    cosine,
    sine,
    mask,
    rows,
    keys,
    values,
    w_sem,
    local_sem,
    ws,
    wr,
    a_s,
    a_r,
    x_s,
    x_r,
    p_s,
    p_r,
    c_s,
    c_r,
    r_s,
    r_r,
    f_s,
    f_r,
):
    p = lax.axis_index("pipe")
    d = lax.axis_index("dp")
    t = lax.axis_index("tensor")
    xl = d % 2
    y = (d // 2) % 4
    z = d // 8

    def at(y_, xl_):
        return (y_ % 4) * 2 + xl_

    def device(slot, pipe=p, z_=z):
        return (pipe, (z_ % 4) * 8 + slot, t)

    own = at(y, xl)

    def nth(j):
        pair, odd = j // 2, j % 2
        along = (pair * (3 - pair)) // 2
        dy = along * (3 + 2 * odd) + 2 * (pair // 3)
        dx = (1 - along) * odd + (pair // 2) * (1 - pair // 3)
        return at(y + dy, (xl + dx) % 2)

    other_core = (p, d, 1 - t)
    partner = device(at(y, 1 - xl))
    y_up, y_down = device(at(y + 1, xl)), device(at(y + 3, xl))
    z_up, z_down = device(own, z_=z + 1), device(own, z_=z + 3)
    across = device(at(y, 1 - xl), pipe=1 - p)

    def weight_copy(step):
        chunk = (step + 8) % CHUNKS
        slot = step % SLOTS
        return pltpu.make_async_copy(
            qkv.at[:, pl.ds(pl.multiple_of(chunk * CHUNK, CHUNK), CHUNK)],
            wbuf.at[slot],
            w_sem.at[slot],
        )

    load_hidden = pltpu.make_async_copy(hidden, x_in, local_sem.at[PIECES])
    small = [
        pltpu.make_async_copy(src, dst, small_sem.at[i])
        for i, (src, dst) in enumerate(
            (
                (seg_in, seg),
                (start_in, start),
                (height_in, height),
                (width_in, width),
                (count_in, count),
                (gain_in, gain),
                (bias_in, bias),
            )
        )
    ]
    for copy in small:
        copy.start()

    @pl.when(p == 0)
    def _():
        load_hidden.start()

    for step in range(AHEAD):
        weight_copy(step).start()
    own_weights = [
        pltpu.make_async_copy(
            out_weight.at[pl.ds(k * PIECE, PIECE)], weights.at[xl, z, k], local_sem.at[k]
        )
        for k in range(PIECES)
    ]

    barrier = pltpu.get_barrier_semaphore()
    pl.semaphore_signal(barrier, inc=1, device_id=other_core, device_id_type=MESH)
    for to in (z_up, z_down):
        pl.semaphore_signal(barrier, inc=1, device_id=to, device_id_type=MESH)
    for j in range(GROUP):
        slot = (own + j) % GROUP
        pl.semaphore_signal(
            barrier, inc=1, device_id=device(slot, pipe=1 - p), device_id_type=MESH
        )
        if j:
            pl.semaphore_signal(barrier, inc=1, device_id=device(slot), device_id_type=MESH)

    def weight_up(k):
        src = out_weight.at[pl.ds(k * PIECE, PIECE)]
        return copy_to(src, weights.at[xl, z, k], ws.at[0, k], wr.at[0, k], z_up)

    def weight_down(k):
        src = out_weight.at[pl.ds(k * PIECE, PIECE)]
        return copy_to(src, weights.at[xl, z, k], ws.at[1, k], wr.at[1, k], z_down)

    def weight_pass_up(k):
        ref = weights.at[xl, (z + 3) % 4, k, pl.ds(0, PIECE // 2)]
        return copy_to(ref, ref, ws.at[2, k], wr.at[2, k], z_up)

    def weight_pass_down(k):
        ref = weights.at[xl, (z + 1) % 4, k, pl.ds(PIECE // 2, PIECE // 2)]
        return copy_to(ref, ref, ws.at[3, k], wr.at[3, k], z_down)

    def weight_over(k):
        src = out_weight.at[pl.ds(k * PIECE, PIECE)]
        return copy_to(src, weights.at[xl, z, k], ws.at[4, k], wr.at[4, k], partner)

    def weight_on(k, kind):
        ref = weights.at[1 - xl, z, k]
        return copy_to(ref, ref, ws.at[kind, k], wr.at[kind, k], z_up if kind == 5 else z_down)

    def weight_opposite(k):
        ref = weights.at[xl, (z + 2) % 4, k]
        return copy_to(ref, ref, ws.at[7, k], wr.at[7, k], partner)

    def pass_weights(k):
        weight_up(k).wait_recv()
        weight_pass_up(k).start()
        weight_down(k).wait_recv()
        weight_pass_down(k).start()

    half = SEQ // 2

    def rows_copy(k, kind):
        ref, to = {
            0: (gathered.at[k, own], partner),
            1: (gathered.at[k, own], y_up),
            2: (gathered.at[k, own], y_down),
            3: (gathered.at[k, at(y, 1 - xl)], y_up),
            4: (gathered.at[k, at(y, 1 - xl)], y_down),
            5: (gathered.at[k, at(y + 3, xl), pl.ds(0, half)], y_up),
            6: (gathered.at[k, at(y + 1, xl), pl.ds(half, half)], y_down),
            7: (gathered.at[k, at(y + 2, xl)], partner),
        }[kind]
        return copy_to(ref, ref, a_s.at[kind, k], a_r.at[kind, k], to)

    def inject(k):
        for kind in (1, 2):
            rows_copy(k, kind).start()

        @pl.when(p == 0)
        def _():
            rows_copy(k, 0).start()

    def pass_first(k):
        rows_copy(k, 0).wait_recv()
        rows_copy(k, 3).start()
        rows_copy(k, 4).start()
        pass_along(k)

    def pass_along(k):
        rows_copy(k, 1).wait_recv()
        rows_copy(k, 5).start()
        rows_copy(k, 2).wait_recv()
        rows_copy(k, 6).start()

    def pass_second(k):
        rows_copy(k, 5).wait_recv()
        rows_copy(k, 6).wait_recv()
        rows_copy(k, 7).start()

    def strip(k):
        return pl.ds(k * (SEQ // PIECES), SEQ // PIECES)

    def send_across(src, k):
        return copy_to(src.at[strip(k)], x_relay.at[strip(k)], r_s.at[k], r_r.at[k], across)

    def pass_across(dst, k):
        return copy_to(x_relay.at[strip(k)], dst.at[strip(k)], f_s.at[k], f_r.at[k], partner)

    for copy in small:
        copy.wait()
    cos, sin, allowed = rotary_tables(seg, start, height, width, count)
    cosine[...] = cos
    sine[...] = sin
    mask[...] = jnp.where(allowed, 1.0, 0.0)
    squares[t] = jnp.zeros((SEQ, 128), jnp.float32)

    def block(slot, zz):
        return pl.ds(pl.multiple_of(zz * 2048 + slot * BLOCK, BLOCK), BLOCK)

    def prepare(slot, zz, update):
        cols = block(slot, zz)
        x = x_in[:, cols]
        if update:
            x = x.astype(jnp.float32) + landed[0, slot, zz].astype(jnp.float32)
            x = x.astype(jnp.bfloat16)
        x_own[:, cols] = x
        x = x.astype(jnp.float32)
        g = gain[:, pl.ds(pl.multiple_of(t * HALF + zz * 2048 + slot * BLOCK, BLOCK), BLOCK)]
        scaled[t, :, cols] = (x * g).astype(jnp.bfloat16)
        x = x * x
        squares[t] += x[:, 0:128] + x[:, 128:256]

    def scaled_copy(slot, zz):
        ref = scaled.at[t, :, block(slot, zz)]
        return copy_to(ref, ref, x_s.at[slot, zz], x_r.at[slot, zz], other_core)

    squares_copy = copy_to(
        squares.at[t], squares.at[t], x_s.at[GROUP, 0], x_r.at[GROUP, 0], other_core
    )
    scaled_whole = copy_to(
        scaled.at[t], scaled.at[t], x_s.at[GROUP, 1], x_r.at[GROUP, 1], other_core
    )

    def landed_wait(layer, slot, zz):
        ref = landed.at[layer, slot, zz]
        pltpu.make_async_copy(ref, ref, c_r.at[layer, slot, zz]).wait()

    def rotated(u):
        return (u * cosine[...] + pltpu.roll(u, HD // 2, 1) * sine[...]).astype(jnp.bfloat16)

    def product(step, core):
        return jnp.dot(
            scaled[core],
            wbuf[step % SLOTS, pl.ds(pl.multiple_of(core * HALF, HALF), HALF)],
            preferred_element_type=jnp.float32,
        )

    def finished(step, u):
        cols = pl.ds(pl.multiple_of(((step + 8) % CHUNKS) * CHUNK, CHUNK), CHUNK)
        scale = rows[...]
        for h in range(2):
            lanes = slice(h * HD, (h + 1) * HD)
            projected[step, :, lanes] = u[:, lanes] * scale + bias[:, cols][:, lanes]

    def first_half(step, carry):
        weight_copy(step).wait()
        projected[step] = product(step, t)
        return carry

    def second_half(step, carry):
        finished(step, projected[step] + product(step, 1 - t))

        @pl.when(step + SLOTS < CHUNKS)
        def _():
            weight_copy(step + SLOTS).start()

        return carry

    def accumulate(core, slot):
        lhs = [scaled[core, :, block(slot, zz)] for zz in range(2)]
        depth = [
            pl.ds(pl.multiple_of(core * HALF + zz * 2048 + slot * BLOCK, BLOCK), BLOCK)
            for zz in range(2)
        ]
        parts = [
            [
                jnp.dot(lhs[zz], wbuf[step, depth[zz]], preferred_element_type=jnp.float32)
                for zz in range(2)
            ]
            for step in range(SLOTS)
        ]
        for step in range(SLOTS):
            projected[step] += parts[step][0] + parts[step][1]

    @pl.when(p == 0)
    def _():
        load_hidden.wait()

        def body(slot, carry):
            for zz in range(2):
                prepare(slot, zz, False)
            return carry

        lax.fori_loop(0, GROUP, body, 0)
        lax.fori_loop(0, EARLY, first_half, 0)

    pl.semaphore_wait(barrier, 2 * GROUP + 2)

    @pl.when(p == 0)
    def _():
        scaled_whole.start()
        squares_copy.start()

    for step in range(AHEAD, SLOTS):
        weight_copy(step).start()
    for k in range(PIECES):
        weight_up(k).start()
        weight_down(k).start()
    for copy in own_weights:
        copy.start()

    @pl.when(p == 0)
    def _():
        for k in range(PIECES):
            send_across(hidden, k).start()

    @pl.when(p == 1)
    def _():
        for k in range(PIECES):
            weight_over(k).start()
        for k in range(PIECES):
            pass_weights(k)
            send_across(hidden, k).wait_recv()
            pass_across(x_in, k).start()
            weight_over(k).wait_recv()
            weight_on(k, 5).start()
            weight_on(k, 6).start()
        for k in range(PIECES):
            weight_pass_up(k).wait_recv()
            weight_pass_down(k).wait_recv()
            weight_opposite(k).start()
        for k in range(PIECES):
            pass_across(x_in, k).wait_recv()

        for step in range(SLOTS):
            weight_copy(step).wait()
            projected[step] = jnp.zeros((SEQ, CHUNK), jnp.float32)

        def from_other(slot):
            for zz in range(2):
                scaled_copy(slot, zz).wait_recv()
            accumulate(1 - t, slot)

        def body(j, carry):
            slot = nth(j)
            for zz in range(2):
                landed_wait(0, slot, zz)
                prepare(slot, zz, True)
                scaled_copy(slot, zz).start()
            accumulate(t, slot)

            @pl.when(j > 1)
            def _():
                from_other(nth(j - 2))

            return carry

        lax.fori_loop(0, GROUP, body, 0)
        squares_copy.start()
        for k in range(PIECES):
            send_across(x_own, k).start()
        from_other(nth(GROUP - 2))
        from_other(nth(GROUP - 1))

    def row_scales():
        squares_copy.wait_recv()
        mean = jnp.sum(squares[0] + squares[1], axis=1, keepdims=True) * (1.0 / D)
        rows[...] = jnp.broadcast_to(lax.rsqrt(mean + EPSILON), (SEQ, SEQ))

    def keys_and_values():
        for h in range(2):
            keys[h] = rotated(projected[0, :, h * HD : (h + 1) * HD])
            values[h] = projected[1, :, h * HD : (h + 1) * HD].astype(jnp.bfloat16)

    def attend(step):
        q_chunk = step - 2
        kv = q_chunk // 4
        for h in range(2):
            scores = lax.dot_general(
                rotated(projected[step, :, h * HD : (h + 1) * HD]),
                keys[kv],
                (((1,), (1,)), ((), ())),
                preferred_element_type=jnp.float32,
            ) * (1.0 / math.sqrt(HD))
            exponent = jnp.where(mask[...] > 0.0, jnp.exp(scores), 0.0)
            weight = exponent * (1.0 / jnp.sum(exponent, axis=1, keepdims=True))
            attended = jnp.dot(
                weight.astype(jnp.bfloat16), values[kv], preferred_element_type=jnp.float32
            )
            cols = pl.multiple_of((q_chunk % 2) * CHUNK + h * HD, HD)
            gathered[q_chunk // 2, own, :, pl.ds(cols, HD)] = attended.astype(jnp.bfloat16)

    def pass_on(q_chunk):
        @pl.when(q_chunk % 2 == 1)
        def _():
            inject(q_chunk // 2)

    def project_second(step, carry):
        attend(step - 1)
        finished(step, projected[step] + product(step, 1 - t))
        pass_on(step - 3)
        return carry

    def project_both(step, carry):
        weight_copy(step).wait()
        attend(step - 1)
        finished(step, product(step, 0) + product(step, 1))
        pass_on(step - 3)
        return carry

    def project_none(step, carry):
        attend(step - 1)
        finished(step, projected[step])
        pass_on(step - 3)
        return carry

    @pl.when(p == 0)
    def _():
        lax.fori_loop(EARLY, SLOTS, first_half, 0)
        row_scales()
        scaled_whole.wait_recv()
        lax.fori_loop(0, 3, second_half, 0)
        keys_and_values()
        lax.fori_loop(3, SLOTS, project_second, 0)

    @pl.when(p == 1)
    def _():
        for step in range(SLOTS, CHUNKS):
            weight_copy(step).start()
        row_scales()
        for step in range(3):
            finished(step, projected[step])
        keys_and_values()
        lax.fori_loop(3, SLOTS, project_none, 0)

    lax.fori_loop(SLOTS, CHUNKS, project_both, 0)
    attend(CHUNKS - 1)
    inject(PIECES - 1)

    def stream_of(e):
        return e + p * (xl - e % 2)

    def place_of(e):
        return own + p * (e % 2 - xl)

    def part_copy(e, zz):
        return copy_to(
            part_out.at[e, zz], part_in.at[e, zz], p_s.at[e, zz], p_r.at[e, zz], other_core
        )

    def sums_copy(e, zz):
        return copy_to(
            sums.at[e, zz],
            landed.at[p, place_of(e), zz],
            c_s.at[e, zz],
            c_r.at[p, place_of(e), zz],
            device(stream_of(e), pipe=1),
        )

    def unit(e, zb):
        stream, xb = stream_of(e), xl + p * (e % 2 - xl)
        part = jnp.dot(gathered[0, stream], weights[xb, zb, 0], preferred_element_type=jnp.float32)
        for k in range(1, PIECES):
            part += jnp.dot(
                gathered[k, stream], weights[xb, zb, k], preferred_element_type=jnp.float32
            )

        @pl.when(zb // 2 == t)
        def _():
            total[e, zb % 2] = part

        @pl.when(zb // 2 != t)
        def _():
            part_out[e, zb % 2] = part.astype(jnp.bfloat16)
            part_copy(e, zb % 2).start()

    def finish(e, zb):
        zz = zb % 2

        @pl.when(zb // 2 == t)
        def _():
            part_copy(e, zz).wait_recv()
            sums[e, zz] = (total[e, zz] + part_in[e, zz].astype(jnp.float32)).astype(jnp.bfloat16)

            @pl.when((p == 0) | (e // 2 != y))
            def _():
                sums_copy(e, zz).start()

    def each(action, count, place):
        def body(i, carry):
            j, turn = place(i)
            action(nth(j), (z + turn) % 4)
            return carry

        lax.fori_loop(0, count, body, 0)

    def each_along(action, dy):
        def body(i, carry):
            action(at(y + dy, (xl + i // 4) % 2), (z + i % 4) % 4)
            return carry

        lax.fori_loop(0, 8, body, 0)

    def near(i):
        return i, 0

    def beside(i):
        return i // 2, 1 + 2 * (i % 2)

    def corner(i):
        return 4 + i // 4, i % 4

    def facing(i):
        return 6, i

    def far(i):
        return i, 2

    def last(i):
        return 7, i

    for copy in own_weights:
        copy.wait()

    @pl.when(p == 0)
    def _():
        pass_first(0)
        pass_weights(0)
        pass_first(1)
        pass_first(2)
        pass_weights(1)
        pass_first(3)
        pass_weights(2)
        each(unit, 4, near)
        pass_weights(3)
        each(finish, 4, near)
        each(unit, 8, beside)
        pass_second(0)
        each(finish, 8, beside)
        pass_second(1)
        for k in range(PIECES):
            weight_pass_up(k).wait_recv()
            weight_pass_down(k).wait_recv()
        each(unit, 4, far)
        each(finish, 4, far)
        pass_second(2)
        pass_second(3)
        for k in range(PIECES):
            rows_copy(k, 3).wait_recv()
            rows_copy(k, 4).wait_recv()
        each(unit, 8, corner)
        each(finish, 8, corner)
        each(unit, 4, facing)
        each(finish, 4, facing)
        for k in range(PIECES):
            rows_copy(k, 7).wait_recv()
        each(unit, 4, last)
        each(finish, 4, last)

    @pl.when(p == 1)
    def _():
        pass_along(0)
        pass_along(1)
        for k in range(PIECES):
            weight_on(k, 5).wait_recv()
            weight_on(k, 6).wait_recv()
            weight_opposite(k).wait_recv()
        each_along(unit, 0)
        pass_along(2)
        pass_along(3)
        each_along(unit, 3)
        each_along(finish, 3)
        each_along(unit, 1)
        each_along(finish, 1)
        for k in range(PIECES):
            rows_copy(k, 5).wait_recv()
            rows_copy(k, 6).wait_recv()
        each_along(unit, 2)
        each_along(finish, 2)
        each_along(finish, 0)

    @pl.when(p == 0)
    def _():
        for k in range(PIECES):
            send_across(x_own, k).wait_recv()
            pass_across(out, k).start()
        for e in range(GROUP):
            for zz in range(2):
                sums_copy(e, zz).wait_send()
        for k in range(PIECES):
            send_across(hidden, k).wait_send()
            pass_across(out, k).wait()
            for kind in (0, 3, 4, 7):
                rows_copy(k, kind).wait_send()
        scaled_whole.wait_send()

    @pl.when(p == 1)
    def _():
        def add(slot, zz, update):
            cols = block(slot, zz)
            out[:, cols] = (
                x_own[:, cols].astype(jnp.float32) + update.astype(jnp.float32)
            ).astype(jnp.bfloat16)

        def body(i, carry):
            slot = at(y + 1 + i // 2, i % 2)
            for zz in range(2):
                landed_wait(1, slot, zz)
                add(slot, zz, landed[1, slot, zz])
            return carry

        for xb in range(2):
            for zz in range(2):
                add(at(y, xb), zz, sums[at(y, xb), zz])
        lax.fori_loop(0, GROUP - 2, body, 0)
        for j in range(2, GROUP):
            for zz in range(2):
                sums_copy((2 * y + j) % GROUP, zz).wait_send()
        for k in range(PIECES):
            send_across(x_own, k).wait_send()
            pass_across(x_in, k).wait_send()
            weight_over(k).wait_send()
            weight_on(k, 5).wait_send()
            weight_on(k, 6).wait_send()
            weight_opposite(k).wait_send()
        for slot in range(GROUP):
            for zz in range(2):
                scaled_copy(slot, zz).wait_send()

    for k in range(PIECES):
        for copy in (weight_up(k), weight_down(k), weight_pass_up(k), weight_pass_down(k)):
            copy.wait_send()
        for kind in (1, 2, 5, 6):
            rows_copy(k, kind).wait_send()
    squares_copy.wait_send()
    for e in range(GROUP):
        for zz in range(2):
            part_copy(e, zz).wait_send()


def local(hidden, gain, qkv, bias, out_weight, segment, start, height, width, count):
    bf16, f32 = jnp.bfloat16, jnp.float32
    anywhere = pl.BlockSpec(memory_space=pl.ANY)
    vmem = pl.BlockSpec(memory_space=pltpu.VMEM)
    dma = pltpu.SemaphoreType.DMA
    result = pl.pallas_call(
        kernel,
        out_shape=jax.ShapeDtypeStruct((SEQ, HALF), bf16),
        in_specs=[anywhere] * 10,
        out_specs=vmem,
        scratch_shapes=[
            pltpu.VMEM(gain.shape, f32),
            pltpu.VMEM(bias.shape, f32),
            pltpu.VMEM(segment.shape, jnp.int32),
            pltpu.SMEM(start.shape, jnp.int32),
            pltpu.SMEM(height.shape, jnp.int32),
            pltpu.SMEM(width.shape, jnp.int32),
            pltpu.SMEM(count.shape, jnp.int32),
            dma((7,)),
            pltpu.VMEM((SLOTS, D, CHUNK), bf16),
            pltpu.VMEM((PIECES, GROUP, SEQ, PIECE), bf16),
            pltpu.VMEM((2, 4, PIECES, PIECE, BLOCK), bf16),
            pltpu.VMEM((2, SEQ, HALF), bf16),
            pltpu.VMEM((2, SEQ, 128), f32),
            pltpu.VMEM((SEQ, HALF), bf16),
            pltpu.VMEM((SEQ, HALF), bf16),
            pltpu.VMEM((SEQ, HALF), bf16),
            pltpu.VMEM((GROUP, 2, SEQ, BLOCK), f32),
            pltpu.VMEM((GROUP, 2, SEQ, BLOCK), bf16),
            pltpu.VMEM((GROUP, 2, SEQ, BLOCK), bf16),
            pltpu.VMEM((GROUP, 2, SEQ, BLOCK), bf16),
            pltpu.VMEM((2, GROUP, 2, SEQ, BLOCK), bf16),
            pltpu.VMEM((CHUNKS, SEQ, CHUNK), f32),
            pltpu.VMEM((SEQ, SEQ), f32),
            pltpu.VMEM((SEQ, SEQ), f32),
            pltpu.VMEM((SEQ, SEQ), f32),
            pltpu.VMEM((SEQ, SEQ), f32),
            pltpu.VMEM((2, SEQ, HD), bf16),
            pltpu.VMEM((2, SEQ, HD), bf16),
            dma((SLOTS,)),
            dma((PIECES + 1,)),
            dma((8, PIECES)),
            dma((8, PIECES)),
            dma((8, PIECES)),
            dma((8, PIECES)),
            dma((GROUP + 1, 2)),
            dma((GROUP + 1, 2)),
            dma((GROUP, 2)),
            dma((GROUP, 2)),
            dma((GROUP, 2)),
            dma((2, GROUP, 2)),
            dma((PIECES,)),
            dma((PIECES,)),
            dma((PIECES,)),
            dma((PIECES,)),
        ],
        compiler_params=pltpu.CompilerParams(
            collective_id=0, has_side_effects=True, vmem_limit_bytes=61 * MIB
        ),
        name="sublayers",
    )(
        hidden[0],
        gain,
        qkv[0],
        bias,
        out_weight[0],
        segment,
        start,
        height,
        width,
        count,
    )
    return result[None, None]


def solution(mesh):
    return jax.shard_map(
        local,
        mesh=mesh,
        in_specs=(
            P(None, "dp", "tensor"),
            P("pipe", None),
            P("pipe", None, "tensor"),
            P("pipe", "tensor"),
            P("pipe", "tensor", "dp"),
            P(None, "dp"),
            P(None, "dp"),
            P(None, "dp"),
            P(None, "dp"),
            P(None, "dp"),
        ),
        out_specs=P("pipe", None, "dp", "tensor"),
        check_vma=False,
    )
```

```python
import math

import jax
import jax.numpy as jnp
from jax import lax
from jax.experimental import pallas as pl
from jax.experimental.pallas import tpu as pltpu
from jax.sharding import PartitionSpec as P

HD = 128
SEQ = 128
D = 8192
HALF = 4096
QUERY = 2048
CHUNK = 256
CHUNKS = 10
SLOTS = 8
EARLY = 1
LAG = 2
AHEAD = 2
PIECES = 4
PIECE = 512
GROUP = 8
BLOCK = 256
THETA = 1000000.0
EPSILON = 1e-06
MIB = 1 << 20
MESH = pl.DeviceIdType.MESH


def copy_to(src, dst, send, recv, device):
    return pltpu.make_async_remote_copy(
        src_ref=src,
        dst_ref=dst,
        send_sem=send,
        recv_sem=recv,
        device_id=device,
        device_id_type=MESH,
    )


def rotary_tables(seg_ref, start_ref, height_ref, width_ref, count_ref):
    row = lax.broadcasted_iota(jnp.int32, (SEQ, SEQ), 0)
    lane = lax.broadcasted_iota(jnp.int32, (SEQ, SEQ), 1)
    seg_keys = jnp.broadcast_to(seg_ref[...].astype(jnp.float32), (SEQ, SEQ))
    seg = jnp.sum(jnp.where(row == lane, seg_keys, 0.0), axis=1, keepdims=True)
    seg = jnp.broadcast_to(seg, (SEQ, SEQ))
    allowed = (row >= lane) & (seg == seg_keys)
    border = jnp.sum(jnp.where(seg_keys == 0.0, 1.0, 0.0), axis=1, keepdims=True)
    first = seg == 0.0

    def choose(ref):
        return jnp.where(
            first, ref[0, 0].astype(jnp.float32), ref[0, 1].astype(jnp.float32)
        )

    begin = jnp.where(first, 0.0, border)
    anchor = choose(start_ref)
    tall = choose(height_ref)
    broad = choose(width_ref)
    present = choose(count_ref)
    counter = row.astype(jnp.float32)
    span = tall * broad * present
    offset = counter - anchor
    inside = (offset >= 0.0) & (offset < span)
    relative = counter - begin
    shifted = relative - span + present * jnp.maximum(tall, broad)
    text = jnp.where(offset >= span, shifted, relative)
    base = anchor - begin
    clipped = jnp.maximum(offset, 0.0)
    grid_row = jnp.floor((clipped + 0.5) / broad)
    grid_col = clipped - grid_row * broad
    freq = lane % (HD // 2)
    inverse = jnp.exp(freq.astype(jnp.float32) * (-2.0 * math.log(THETA) / HD))
    moved = jnp.where(
        freq < HD // 8, 0.0, jnp.where(freq < HD // 8 + 3 * HD // 16, grid_row, grid_col)
    )
    angles = jnp.where(inside, base + moved, text) * inverse
    sine = jnp.sin(angles)
    return jnp.cos(angles), jnp.where(lane < HD // 2, -sine, sine), allowed


def kernel(
    hidden,
    gain_in,
    qkv,
    bias_in,
    out_weight,
    seg_in,
    start_in,
    height_in,
    width_in,
    count_in,
    out,
    gain,
    bias,
    seg,
    start,
    height,
    width,
    count,
    small_sem,
    wbuf,
    gathered,
    weights,
    scaled,
    squares,
    x_own,
    x_in,
    x_relay,
    total,
    part_out,
    part_in,
    sums,
    landed,
    projected,
    cosine,
    sine,
    mask,
    rows,
    keys,
    values,
    w_sem,
    local_sem,
    ws,
    wr,
    a_s,
    a_r,
    x_s,
    x_r,
    p_s,
    p_r,
    c_s,
    c_r,
    r_s,
    r_r,
    f_s,
    f_r,
):
    p = lax.axis_index("pipe")
    d = lax.axis_index("dp")
    t = lax.axis_index("tensor")
    xl = d % 2
    y = (d // 2) % 4
    z = d // 8

    def at(y_, xl_):
        return (y_ % 4) * 2 + xl_

    def device(slot, pipe=p, z_=z):
        return (pipe, (z_ % 4) * 8 + slot, t)

    own = at(y, xl)

    def nth(j):
        pair, odd = j // 2, j % 2
        along = (pair * (3 - pair)) // 2
        dy = along * (3 + 2 * odd) + 2 * (pair // 3)
        dx = (1 - along) * odd + (pair // 2) * (1 - pair // 3)
        return at(y + dy, (xl + dx) % 2)

    other_core = (p, d, 1 - t)
    partner = device(at(y, 1 - xl))
    y_up, y_down = device(at(y + 1, xl)), device(at(y + 3, xl))
    z_up, z_down = device(own, z_=z + 1), device(own, z_=z + 3)
    across = device(at(y, 1 - xl), pipe=1 - p)

    def weight_copy(step):
        chunk = (step + 8) % CHUNKS
        slot = step % SLOTS
        return pltpu.make_async_copy(
            qkv.at[:, pl.ds(pl.multiple_of(chunk * CHUNK, CHUNK), CHUNK)],
            wbuf.at[slot],
            w_sem.at[slot],
        )

    load_hidden = pltpu.make_async_copy(hidden, x_in, local_sem.at[PIECES])
    small = [
        pltpu.make_async_copy(src, dst, small_sem.at[i])
        for i, (src, dst) in enumerate(
            (
                (seg_in, seg),
                (start_in, start),
                (height_in, height),
                (width_in, width),
                (count_in, count),
                (gain_in, gain),
                (bias_in, bias),
            )
        )
    ]
    for copy in small:
        copy.start()

    @pl.when(p == 0)
    def _():
        load_hidden.start()

    for step in range(AHEAD):
        weight_copy(step).start()
    own_weights = [
        pltpu.make_async_copy(
            out_weight.at[pl.ds(k * PIECE, PIECE)], weights.at[xl, z, k], local_sem.at[k]
        )
        for k in range(PIECES)
    ]

    barrier = pltpu.get_barrier_semaphore()
    pl.semaphore_signal(barrier, inc=1, device_id=other_core, device_id_type=MESH)
    for to in (z_up, z_down):
        pl.semaphore_signal(barrier, inc=1, device_id=to, device_id_type=MESH)
    for j in range(GROUP):
        slot = (own + j) % GROUP
        pl.semaphore_signal(
            barrier, inc=1, device_id=device(slot, pipe=1 - p), device_id_type=MESH
        )
        if j:
            pl.semaphore_signal(barrier, inc=1, device_id=device(slot), device_id_type=MESH)

    def weight_up(k):
        src = out_weight.at[pl.ds(k * PIECE, PIECE)]
        return copy_to(src, weights.at[xl, z, k], ws.at[0, k], wr.at[0, k], z_up)

    def weight_down(k):
        src = out_weight.at[pl.ds(k * PIECE, PIECE)]
        return copy_to(src, weights.at[xl, z, k], ws.at[1, k], wr.at[1, k], z_down)

    def weight_pass_up(k):
        ref = weights.at[xl, (z + 3) % 4, k, pl.ds(0, PIECE // 2)]
        return copy_to(ref, ref, ws.at[2, k], wr.at[2, k], z_up)

    def weight_pass_down(k):
        ref = weights.at[xl, (z + 1) % 4, k, pl.ds(PIECE // 2, PIECE // 2)]
        return copy_to(ref, ref, ws.at[3, k], wr.at[3, k], z_down)

    def weight_over(k):
        src = out_weight.at[pl.ds(k * PIECE, PIECE)]
        return copy_to(src, weights.at[xl, z, k], ws.at[4, k], wr.at[4, k], partner)

    def weight_on(k, kind):
        ref = weights.at[1 - xl, z, k]
        return copy_to(ref, ref, ws.at[kind, k], wr.at[kind, k], z_up if kind == 5 else z_down)

    def weight_opposite(k):
        ref = weights.at[xl, (z + 2) % 4, k]
        return copy_to(ref, ref, ws.at[7, k], wr.at[7, k], partner)

    def pass_weights(k):
        weight_up(k).wait_recv()
        weight_pass_up(k).start()
        weight_down(k).wait_recv()
        weight_pass_down(k).start()

    half = SEQ // 2

    def rows_copy(k, kind):
        ref, to = {
            0: (gathered.at[k, own], partner),
            1: (gathered.at[k, own], y_up),
            2: (gathered.at[k, own], y_down),
            3: (gathered.at[k, at(y, 1 - xl)], y_up),
            4: (gathered.at[k, at(y, 1 - xl)], y_down),
            5: (gathered.at[k, at(y + 3, xl), pl.ds(0, half)], y_up),
            6: (gathered.at[k, at(y + 1, xl), pl.ds(half, half)], y_down),
            7: (gathered.at[k, at(y + 2, xl)], partner),
        }[kind]
        return copy_to(ref, ref, a_s.at[kind, k], a_r.at[kind, k], to)

    def inject(k):
        for kind in (1, 2):
            rows_copy(k, kind).start()

        @pl.when(p == 0)
        def _():
            rows_copy(k, 0).start()

    def pass_first(k):
        rows_copy(k, 0).wait_recv()
        rows_copy(k, 3).start()
        rows_copy(k, 4).start()
        pass_along(k)

    def pass_along(k):
        rows_copy(k, 1).wait_recv()
        rows_copy(k, 5).start()
        rows_copy(k, 2).wait_recv()
        rows_copy(k, 6).start()

    def pass_second(k):
        rows_copy(k, 5).wait_recv()
        rows_copy(k, 6).wait_recv()
        rows_copy(k, 7).start()

    def strip(k):
        return pl.ds(k * (SEQ // PIECES), SEQ // PIECES)

    def send_across(src, k):
        return copy_to(src.at[strip(k)], x_relay.at[strip(k)], r_s.at[k], r_r.at[k], across)

    def pass_across(dst, k):
        return copy_to(x_relay.at[strip(k)], dst.at[strip(k)], f_s.at[k], f_r.at[k], partner)

    for copy in small:
        copy.wait()
    cos, sin, allowed = rotary_tables(seg, start, height, width, count)
    cosine[...] = cos
    sine[...] = sin
    mask[...] = jnp.where(allowed, 1.0, 0.0)
    squares[t] = jnp.zeros((SEQ, 128), jnp.float32)

    def block(slot, zz):
        return pl.ds(pl.multiple_of(zz * 2048 + slot * BLOCK, BLOCK), BLOCK)

    def prepare(slot, zz, update):
        cols = block(slot, zz)
        x = x_in[:, cols]
        if update:
            x = x.astype(jnp.float32) + landed[0, slot, zz].astype(jnp.float32)
            x = x.astype(jnp.bfloat16)
        x_own[:, cols] = x
        x = x.astype(jnp.float32)
        g = gain[:, pl.ds(pl.multiple_of(t * HALF + zz * 2048 + slot * BLOCK, BLOCK), BLOCK)]
        scaled[t, :, cols] = (x * g).astype(jnp.bfloat16)
        x = x * x
        squares[t] += x[:, 0:128] + x[:, 128:256]

    def scaled_copy(slot, zz):
        ref = scaled.at[t, :, block(slot, zz)]
        return copy_to(ref, ref, x_s.at[slot, zz], x_r.at[slot, zz], other_core)

    squares_copy = copy_to(
        squares.at[t], squares.at[t], x_s.at[GROUP, 0], x_r.at[GROUP, 0], other_core
    )
    scaled_whole = copy_to(
        scaled.at[t], scaled.at[t], x_s.at[GROUP, 1], x_r.at[GROUP, 1], other_core
    )

    def landed_wait(layer, slot, zz):
        ref = landed.at[layer, slot, zz]
        pltpu.make_async_copy(ref, ref, c_r.at[layer, slot, zz]).wait()

    def rotated(u):
        return (u * cosine[...] + pltpu.roll(u, HD // 2, 1) * sine[...]).astype(jnp.bfloat16)

    def product(step, core):
        return jnp.dot(
            scaled[core],
            wbuf[step % SLOTS, pl.ds(pl.multiple_of(core * HALF, HALF), HALF)],
            preferred_element_type=jnp.float32,
        )

    def finished(step, u):
        cols = pl.ds(pl.multiple_of(((step + 8) % CHUNKS) * CHUNK, CHUNK), CHUNK)
        scale = rows[...]
        for h in range(2):
            lanes = slice(h * HD, (h + 1) * HD)
            projected[step, :, lanes] = u[:, lanes] * scale + bias[:, cols][:, lanes]

    def first_half(step, carry):
        weight_copy(step).wait()
        projected[step] = product(step, t)
        return carry

    def second_half(step, carry):
        finished(step, projected[step] + product(step, 1 - t))

        @pl.when(step + SLOTS < CHUNKS)
        def _():
            weight_copy(step + SLOTS).start()

        return carry

    def accumulate(core, slot):
        lhs = [scaled[core, :, block(slot, zz)] for zz in range(2)]
        depth = [
            pl.ds(pl.multiple_of(core * HALF + zz * 2048 + slot * BLOCK, BLOCK), BLOCK)
            for zz in range(2)
        ]
        parts = [
            [
                jnp.dot(lhs[zz], wbuf[step, depth[zz]], preferred_element_type=jnp.float32)
                for zz in range(2)
            ]
            for step in range(SLOTS)
        ]
        for step in range(SLOTS):
            projected[step] += parts[step][0] + parts[step][1]

    @pl.when(p == 0)
    def _():
        load_hidden.wait()

        def body(slot, carry):
            for zz in range(2):
                prepare(slot, zz, False)
            return carry

        lax.fori_loop(0, GROUP, body, 0)
        lax.fori_loop(0, EARLY, first_half, 0)

    pl.semaphore_wait(barrier, 2 * GROUP + 2)

    @pl.when(p == 0)
    def _():
        scaled_whole.start()
        squares_copy.start()

    for step in range(AHEAD, SLOTS):
        weight_copy(step).start()
    for k in range(PIECES):
        weight_up(k).start()
        weight_down(k).start()
    for copy in own_weights:
        copy.start()

    @pl.when(p == 0)
    def _():
        for k in range(PIECES):
            send_across(hidden, k).start()

    @pl.when(p == 1)
    def _():
        for k in range(PIECES):
            weight_over(k).start()
        for k in range(PIECES):
            pass_weights(k)
            send_across(hidden, k).wait_recv()
            pass_across(x_in, k).start()
            weight_over(k).wait_recv()
            weight_on(k, 5).start()
            weight_on(k, 6).start()
        for k in range(PIECES):
            weight_pass_up(k).wait_recv()
            weight_pass_down(k).wait_recv()
            weight_opposite(k).start()
        for k in range(PIECES):
            pass_across(x_in, k).wait_recv()

        for step in range(SLOTS):
            weight_copy(step).wait()
            projected[step] = jnp.zeros((SEQ, CHUNK), jnp.float32)

        def from_other(slot):
            for zz in range(2):
                scaled_copy(slot, zz).wait_recv()
            accumulate(1 - t, slot)

        def body(j, carry):
            slot = nth(j)
            for zz in range(2):
                landed_wait(0, slot, zz)
                prepare(slot, zz, True)
                scaled_copy(slot, zz).start()
            accumulate(t, slot)

            @pl.when(j > 1)
            def _():
                from_other(nth(j - 2))

            return carry

        lax.fori_loop(0, GROUP, body, 0)
        squares_copy.start()
        for k in range(PIECES):
            send_across(x_own, k).start()
        from_other(nth(GROUP - 2))
        from_other(nth(GROUP - 1))

    def row_scales():
        squares_copy.wait_recv()
        mean = jnp.sum(squares[0] + squares[1], axis=1, keepdims=True) * (1.0 / D)
        rows[...] = jnp.broadcast_to(lax.rsqrt(mean + EPSILON), (SEQ, SEQ))

    def keys_and_values():
        for h in range(2):
            keys[h] = rotated(projected[0, :, h * HD : (h + 1) * HD])
            values[h] = projected[1, :, h * HD : (h + 1) * HD].astype(jnp.bfloat16)

    def attend(step):
        q_chunk = step - 2
        kv = q_chunk // 4
        for h in range(2):
            scores = lax.dot_general(
                rotated(projected[step, :, h * HD : (h + 1) * HD]),
                keys[kv],
                (((1,), (1,)), ((), ())),
                preferred_element_type=jnp.float32,
            ) * (1.0 / math.sqrt(HD))
            exponent = jnp.where(mask[...] > 0.0, jnp.exp(scores), 0.0)
            weight = exponent * (1.0 / jnp.sum(exponent, axis=1, keepdims=True))
            attended = jnp.dot(
                weight.astype(jnp.bfloat16), values[kv], preferred_element_type=jnp.float32
            )
            cols = pl.multiple_of((q_chunk % 2) * CHUNK + h * HD, HD)
            gathered[q_chunk // 2, own, :, pl.ds(cols, HD)] = attended.astype(jnp.bfloat16)

    def pass_on(q_chunk):
        @pl.when(q_chunk % 2 == 1)
        def _():
            inject(q_chunk // 2)

    def project_second(step, carry):
        attend(step - 1)
        finished(step, projected[step] + product(step, 1 - t))
        pass_on(step - 3)
        return carry

    def project_both(step, carry):
        weight_copy(step).wait()
        attend(step - 1)
        finished(step, product(step, 0) + product(step, 1))
        pass_on(step - 3)
        return carry

    def project_none(step, carry):
        attend(step - 1)
        finished(step, projected[step])
        pass_on(step - 3)
        return carry

    @pl.when(p == 0)
    def _():
        lax.fori_loop(EARLY, SLOTS, first_half, 0)
        row_scales()
        scaled_whole.wait_recv()
        lax.fori_loop(0, 3, second_half, 0)
        keys_and_values()
        lax.fori_loop(3, SLOTS, project_second, 0)

    @pl.when(p == 1)
    def _():
        for step in range(SLOTS, CHUNKS):
            weight_copy(step).start()
        row_scales()
        for step in range(3):
            finished(step, projected[step])
        keys_and_values()
        lax.fori_loop(3, SLOTS, project_none, 0)

    lax.fori_loop(SLOTS, CHUNKS, project_both, 0)
    attend(CHUNKS - 1)
    inject(PIECES - 1)

    def stream_of(e):
        return e + p * (xl - e % 2)

    def place_of(e):
        return own + p * (e % 2 - xl)

    def part_copy(e, zz):
        return copy_to(
            part_out.at[e, zz], part_in.at[e, zz], p_s.at[e, zz], p_r.at[e, zz], other_core
        )

    def sums_copy(e, zz):
        return copy_to(
            sums.at[e, zz],
            landed.at[p, place_of(e), zz],
            c_s.at[e, zz],
            c_r.at[p, place_of(e), zz],
            device(stream_of(e), pipe=1),
        )

    def unit(e, zb):
        stream, xb = stream_of(e), xl + p * (e % 2 - xl)
        part = jnp.dot(gathered[0, stream], weights[xb, zb, 0], preferred_element_type=jnp.float32)
        for k in range(1, PIECES):
            part += jnp.dot(
                gathered[k, stream], weights[xb, zb, k], preferred_element_type=jnp.float32
            )

        @pl.when(zb // 2 == t)
        def _():
            total[e, zb % 2] = part

        @pl.when(zb // 2 != t)
        def _():
            part_out[e, zb % 2] = part.astype(jnp.bfloat16)
            part_copy(e, zb % 2).start()

    def finish(e, zb):
        zz = zb % 2

        @pl.when(zb // 2 == t)
        def _():
            part_copy(e, zz).wait_recv()
            sums[e, zz] = (total[e, zz] + part_in[e, zz].astype(jnp.float32)).astype(jnp.bfloat16)

            @pl.when((p == 0) | (e // 2 != y))
            def _():
                sums_copy(e, zz).start()

    def each(action, count, place):
        def body(i, carry):
            j, turn = place(i)
            action(nth(j), (z + turn) % 4)
            return carry

        lax.fori_loop(0, count, body, 0)

    def each_along(action, dy):
        def body(i, carry):
            action(at(y + dy, (xl + i // 4) % 2), (z + i % 4) % 4)
            return carry

        lax.fori_loop(0, 8, body, 0)

    def staggered(count, entry):
        def body(i, carry):
            @pl.when(i < count)
            def _():
                unit(*entry(i))

            @pl.when(i >= LAG)
            def _():
                finish(*entry(i - LAG))

            return carry

        lax.fori_loop(0, count + LAG, body, 0)

    def staggered_each(count, place):
        def entry(i):
            j, turn = place(i)
            return nth(j), (z + turn) % 4

        staggered(count, entry)

    def staggered_along(dy):
        staggered(8, lambda i: (at(y + dy, (xl + i // 4) % 2), (z + i % 4) % 4))

    def near(i):
        return i, 0

    def beside(i):
        return i // 2, 1 + 2 * (i % 2)

    def corner(i):
        return 4 + i // 4, i % 4

    def facing(i):
        return 6, i

    def far(i):
        return i, 2

    def last(i):
        return 7, i

    for copy in own_weights:
        copy.wait()

    @pl.when(p == 0)
    def _():
        pass_first(0)
        pass_weights(0)
        pass_first(1)
        pass_first(2)
        pass_weights(1)
        pass_first(3)
        pass_weights(2)
        each(unit, 4, near)
        pass_weights(3)
        each(finish, 4, near)
        each(unit, 8, beside)
        pass_second(0)
        each(finish, 8, beside)
        pass_second(1)
        for k in range(PIECES):
            weight_pass_up(k).wait_recv()
            weight_pass_down(k).wait_recv()
        staggered_each(4, far)
        pass_second(2)
        pass_second(3)
        for k in range(PIECES):
            rows_copy(k, 3).wait_recv()
            rows_copy(k, 4).wait_recv()
        staggered_each(8, corner)
        staggered_each(4, facing)
        for k in range(PIECES):
            rows_copy(k, 7).wait_recv()
        staggered_each(4, last)

    @pl.when(p == 1)
    def _():
        pass_along(0)
        pass_along(1)
        for k in range(PIECES):
            weight_on(k, 5).wait_recv()
            weight_on(k, 6).wait_recv()
            weight_opposite(k).wait_recv()
        each_along(unit, 0)
        pass_along(2)
        pass_along(3)
        staggered_along(3)
        staggered_along(1)
        for k in range(PIECES):
            rows_copy(k, 5).wait_recv()
            rows_copy(k, 6).wait_recv()
        staggered_along(2)
        each_along(finish, 0)

    @pl.when(p == 0)
    def _():
        for k in range(PIECES):
            send_across(x_own, k).wait_recv()
            pass_across(out, k).start()
        for e in range(GROUP):
            for zz in range(2):
                sums_copy(e, zz).wait_send()
        for k in range(PIECES):
            send_across(hidden, k).wait_send()
            pass_across(out, k).wait()
            for kind in (0, 3, 4, 7):
                rows_copy(k, kind).wait_send()
        scaled_whole.wait_send()

    @pl.when(p == 1)
    def _():
        def add(slot, zz, update):
            cols = block(slot, zz)
            out[:, cols] = (
                x_own[:, cols].astype(jnp.float32) + update.astype(jnp.float32)
            ).astype(jnp.bfloat16)

        def body(i, carry):
            slot = at(y + 1 + i // 2, i % 2)
            for zz in range(2):
                landed_wait(1, slot, zz)
                add(slot, zz, landed[1, slot, zz])
            return carry

        for xb in range(2):
            for zz in range(2):
                add(at(y, xb), zz, sums[at(y, xb), zz])
        lax.fori_loop(0, GROUP - 2, body, 0)
        for j in range(2, GROUP):
            for zz in range(2):
                sums_copy((2 * y + j) % GROUP, zz).wait_send()
        for k in range(PIECES):
            send_across(x_own, k).wait_send()
            pass_across(x_in, k).wait_send()
            weight_over(k).wait_send()
            weight_on(k, 5).wait_send()
            weight_on(k, 6).wait_send()
            weight_opposite(k).wait_send()
        for slot in range(GROUP):
            for zz in range(2):
                scaled_copy(slot, zz).wait_send()

    for k in range(PIECES):
        for copy in (weight_up(k), weight_down(k), weight_pass_up(k), weight_pass_down(k)):
            copy.wait_send()
        for kind in (1, 2, 5, 6):
            rows_copy(k, kind).wait_send()
    squares_copy.wait_send()
    for e in range(GROUP):
        for zz in range(2):
            part_copy(e, zz).wait_send()


def local(hidden, gain, qkv, bias, out_weight, segment, start, height, width, count):
    bf16, f32 = jnp.bfloat16, jnp.float32
    anywhere = pl.BlockSpec(memory_space=pl.ANY)
    vmem = pl.BlockSpec(memory_space=pltpu.VMEM)
    dma = pltpu.SemaphoreType.DMA
    result = pl.pallas_call(
        kernel,
        out_shape=jax.ShapeDtypeStruct((SEQ, HALF), bf16),
        in_specs=[anywhere] * 10,
        out_specs=vmem,
        scratch_shapes=[
            pltpu.VMEM(gain.shape, f32),
            pltpu.VMEM(bias.shape, f32),
            pltpu.VMEM(segment.shape, jnp.int32),
            pltpu.SMEM(start.shape, jnp.int32),
            pltpu.SMEM(height.shape, jnp.int32),
            pltpu.SMEM(width.shape, jnp.int32),
            pltpu.SMEM(count.shape, jnp.int32),
            dma((7,)),
            pltpu.VMEM((SLOTS, D, CHUNK), bf16),
            pltpu.VMEM((PIECES, GROUP, SEQ, PIECE), bf16),
            pltpu.VMEM((2, 4, PIECES, PIECE, BLOCK), bf16),
            pltpu.VMEM((2, SEQ, HALF), bf16),
            pltpu.VMEM((2, SEQ, 128), f32),
            pltpu.VMEM((SEQ, HALF), bf16),
            pltpu.VMEM((SEQ, HALF), bf16),
            pltpu.VMEM((SEQ, HALF), bf16),
            pltpu.VMEM((GROUP, 2, SEQ, BLOCK), f32),
            pltpu.VMEM((GROUP, 2, SEQ, BLOCK), bf16),
            pltpu.VMEM((GROUP, 2, SEQ, BLOCK), bf16),
            pltpu.VMEM((GROUP, 2, SEQ, BLOCK), bf16),
            pltpu.VMEM((2, GROUP, 2, SEQ, BLOCK), bf16),
            pltpu.VMEM((CHUNKS, SEQ, CHUNK), f32),
            pltpu.VMEM((SEQ, SEQ), f32),
            pltpu.VMEM((SEQ, SEQ), f32),
            pltpu.VMEM((SEQ, SEQ), f32),
            pltpu.VMEM((SEQ, SEQ), f32),
            pltpu.VMEM((2, SEQ, HD), bf16),
            pltpu.VMEM((2, SEQ, HD), bf16),
            dma((SLOTS,)),
            dma((PIECES + 1,)),
            dma((8, PIECES)),
            dma((8, PIECES)),
            dma((8, PIECES)),
            dma((8, PIECES)),
            dma((GROUP + 1, 2)),
            dma((GROUP + 1, 2)),
            dma((GROUP, 2)),
            dma((GROUP, 2)),
            dma((GROUP, 2)),
            dma((2, GROUP, 2)),
            dma((PIECES,)),
            dma((PIECES,)),
            dma((PIECES,)),
            dma((PIECES,)),
        ],
        compiler_params=pltpu.CompilerParams(
            collective_id=0, has_side_effects=True, vmem_limit_bytes=61 * MIB
        ),
        name="sublayers",
    )(
        hidden[0],
        gain,
        qkv[0],
        bias,
        out_weight[0],
        segment,
        start,
        height,
        width,
        count,
    )
    return result[None, None]


def solution(mesh):
    return jax.shard_map(
        local,
        mesh=mesh,
        in_specs=(
            P(None, "dp", "tensor"),
            P("pipe", None),
            P("pipe", None, "tensor"),
            P("pipe", "tensor"),
            P("pipe", "tensor", "dp"),
            P(None, "dp"),
            P(None, "dp"),
            P(None, "dp"),
            P(None, "dp"),
            P(None, "dp"),
        ),
        out_specs=P("pipe", None, "dp", "tensor"),
        check_vma=False,
    )
```
